256 devices in a mesh: leaf: 64 (over z, y, core), sub: 4 (over x).
Axes of the slice: x: 4, y: 4, z: 8, core: 2. Of those that a mesh axis runs over, the one named last changes fastest.
Arguments:
- probes: bfloat16 [32, 1024, 256], P(None, 'leaf', 'sub'), may hold values from -6 to 6
- near_blocks: bfloat16 [1024, 9, 256, 256], P('leaf', None, 'sub'), may hold values from -0.125 to 0.125
- leaf_cluster_basis: bfloat16 [1024, 64, 256], P('leaf', None, 'sub'), may hold values from -0.375 to 0.375
- transfer: bfloat16 [1024, 64, 64], P('leaf'), may hold values from -0.375 to 0.375
- couplings: bfloat16 [1024, 16, 64, 64], P('leaf'), may hold values from -0.1875 to 0.1875
- coarse_couplings: bfloat16 [256, 16, 64, 64], P('leaf'), may hold values from -0.1875 to 0.1875
- near_list: int32 [1024, 9], P('leaf'), may hold values from -1 to 1023, as said below
- distant_interaction_list: int32 [1024, 16], P('leaf'), may hold values from -1 to 1023, as said below
- coarse_list: int32 [256, 16], P('leaf'), may hold values from -1 to 255, as said below
Outputs:
- first_apply: bfloat16 [32, 1024, 256], P(None, 'leaf', 'sub')
- second_apply: bfloat16 [32, 1024, 256], P(None, 'leaf', 'sub')
The draws below stay inside these ranges and needn't reach their ends.
Inputs may be any that keep to these rules, and one draw needn't show every extreme that they name: `near_list`: slot 0 of leaf i holds i; every other entry is -1 (an unused slot) or a leaf at most 4 positions from i in tree order. `distant_interaction_list`: entries are -1 (an unused slot) or leaves. The 16 leaves of one index of leaf name, over all their slots, at most 2 distinct leaves of any one index of leaf (itself included), and in every draw some index names exactly 2 leaves of another. `coarse_list`: entries are -1 (an unused slot) or parent clusters.
All inputs are finite; a program needn't handle non-finite values.
Results may differ from the reference program's by a relative error of at most 0.009.
Values may be sent and summed in bfloat16 or wider, within the bound.
No kernel may reach another device: no remote copies, remote signals or barrier semaphores. Data moves between devices by JAX's collectives and lax.ppermute only.
A program may use at most 64 MiB of HBM per device.

```python
import jax
import jax.numpy as jnp
from jax import lax

LEAF = 256
RANK = 64
PROBES = 32
LEAF_DEV = 16
NEAR = 9
FAR = 16
CFAR = 16
BRANCH = 4
REACH = 4
CAP = 2
LEAVES = 1024
PARENTS = 256


def draw_near_list(key, part):
    key = jax.random.fold_in(key, 11)
    key_offset, key_count = jax.random.split(key)
    leaf_ids = jnp.arange(LEAVES, dtype=jnp.int32)[:, None]
    offsets = jax.random.randint(key_offset, (LEAVES, NEAR), -REACH, REACH + 1, dtype=jnp.int32)
    counts = jax.random.randint(key_count, (LEAVES, 1), 3, NEAR + 1, dtype=jnp.int32)
    slots = jnp.arange(NEAR, dtype=jnp.int32)[None, :]
    target = jnp.clip(leaf_ids + offsets, 0, LEAVES - 1)
    target = jnp.where(slots == 0, leaf_ids, target)
    return jnp.where(slots < counts, target, -1).astype(jnp.int32)


def draw_distant_interaction_list(key, part):
    key = jax.random.fold_in(key, 12)
    key_peer, key_start, key_step, key_live = jax.random.split(key, 4)
    groups = LEAVES // LEAF_DEV
    leaf_ids = jnp.arange(LEAVES, dtype=jnp.int32)
    owner = leaf_ids // LEAF_DEV
    peers = jax.random.randint(key_peer, (LEAVES, FAR), 0, groups, dtype=jnp.int32)
    starts = jax.random.randint(key_start, (groups, groups), 0, LEAF_DEV, dtype=jnp.int32)
    steps = jax.random.randint(key_step, (LEAVES, FAR), 0, CAP, dtype=jnp.int32)
    living = jax.random.randint(key_live, (LEAVES, FAR), 0, 4, dtype=jnp.int32) > 0
    slots = jnp.arange(FAR, dtype=jnp.int32)[None, :]
    forced = (leaf_ids % LEAF_DEV == 0)[:, None] & (slots < CAP)
    peers = jnp.where(forced, ((owner + 1) % groups)[:, None], peers)
    steps = jnp.where(forced, slots, steps)
    living = living | forced
    local = (starts[owner[:, None], peers] + steps) % LEAF_DEV
    target = peers * LEAF_DEV + local
    return jnp.where(living, target, -1).astype(jnp.int32)


def draw_coarse_list(key, part):
    key = jax.random.fold_in(key, 13)
    key_target, key_live = jax.random.split(key)
    target = jax.random.randint(key_target, (PARENTS, CFAR), 0, PARENTS, dtype=jnp.int32)
    living = jax.random.randint(key_live, (PARENTS, CFAR), 0, 4, dtype=jnp.int32) > 0
    return jnp.where(living, target, -1).astype(jnp.int32)


def shard_levels(key, dims, shards, low, top_value):
    gain, own = 1.0, jax.random.fold_in(key, 6)
    for dim, parts in shards:
        steps = jnp.exp(jax.random.uniform(jax.random.fold_in(own, dim), (parts,), jnp.float32, low / len(shards), top_value / len(shards)))
        gain = gain * jnp.repeat(steps, dims[dim] // parts).reshape([-1 if axis == dim else 1 for axis in range(len(dims))])
    return gain


def normal_values(key, shape, scale, reach, cuts=(), held_as=jnp.bfloat16):
    result = scale * jax.random.normal(key, shape, jnp.float32)
    if cuts:
        result = result * shard_levels(key, shape, cuts, -0.22, 0.18)
    return jnp.clip(result, -reach, reach).astype(held_as)


def setup_inputs(seed: int = 0) -> dict:
    streams_of = jax.random.split(jax.random.key(seed), 10)
    probes = normal_values(streams_of[0], (PROBES, LEAVES, LEAF), 1.0, 6.0, ((1, 64), (2, 4)))
    near_blocks = normal_values(streams_of[1], (LEAVES, NEAR, LEAF, LEAF), (LEAF * NEAR) ** -0.5, 0.125, ((0, 64), (2, 4)))
    leaf_cluster_basis = normal_values(streams_of[2], (LEAVES, RANK, LEAF), LEAF ** -0.5, 0.375, ((0, 64), (2, 4)))
    transfer = normal_values(streams_of[3], (LEAVES, RANK, RANK), (RANK * BRANCH) ** -0.5, 0.375, ((0, 64),))
    couplings = normal_values(streams_of[4], (LEAVES, FAR, RANK, RANK), (RANK * FAR) ** -0.5, 0.1875, ((0, 64),))
    coarse_couplings = normal_values(streams_of[5], (PARENTS, CFAR, RANK, RANK), (RANK * CFAR) ** -0.5, 0.1875, ((0, 64),))
    near_list = draw_near_list(jax.random.fold_in(streams_of[9], 71), 0)
    distant_interaction_list = draw_distant_interaction_list(jax.random.fold_in(streams_of[9], 71), 0)
    coarse_list = draw_coarse_list(jax.random.fold_in(streams_of[9], 71), 0)
    return {"probes": probes, "near_blocks": near_blocks, "leaf_cluster_basis": leaf_cluster_basis, "transfer": transfer, "couplings": couplings, "coarse_couplings": coarse_couplings, "near_list": near_list, "distant_interaction_list": distant_interaction_list, "coarse_list": coarse_list}


def near_leaf(probe_vector_batch):
    def compute(items):
        blocks, indices, flags = items
        chosen = jnp.take(probe_vector_batch, indices, axis=1)
        chosen = jnp.where(flags[None, :, None], chosen, jnp.zeros_like(chosen))
        left_side = chosen.reshape(PROBES, NEAR * LEAF).astype(jnp.float32)
        right_side = jnp.transpose(blocks, (0, 2, 1)).reshape(NEAR * LEAF, LEAF).astype(jnp.float32)
        return jnp.dot(left_side, right_side, precision=lax.Precision.HIGHEST)
    return compute


def couple(coefs, weights, listing):
    live_entries = listing >= 0
    picked = coefs[jnp.where(live_entries, listing, 0)]
    picked = jnp.where(live_entries[:, :, None, None], picked, jnp.zeros_like(picked))
    return jnp.einsum("ikab,ikbp->iap", weights.astype(jnp.float32), picked.astype(jnp.float32), precision=lax.Precision.HIGHEST)


def apply_once(probe_vector_batch, near_blocks, leaf_cluster_basis, transfer, couplings, coarse_couplings, near_list, distant_interaction_list, coarse_list):
    live_near = near_list >= 0
    safe_near = jnp.where(live_near, near_list, 0)
    near_part = lax.map(near_leaf(probe_vector_batch), (near_blocks, safe_near, live_near))
    near_part = jnp.transpose(near_part, (1, 0, 2))
    broad_basis_matrix = leaf_cluster_basis.astype(jnp.float32)
    transfer_wide = transfer.astype(jnp.float32)
    leaf_level_sums = jnp.einsum("dze,sde->dzs", broad_basis_matrix, probe_vector_batch.astype(jnp.float32), precision=lax.Precision.HIGHEST)
    parent_sums = jnp.einsum("iab,iap->ibp", transfer_wide, leaf_level_sums, precision=lax.Precision.HIGHEST)
    parent_sums = parent_sums.reshape(PARENTS, BRANCH, RANK, PROBES).sum(axis=1)
    leaf_coef = leaf_level_sums.astype(jnp.bfloat16)
    parent_coef = parent_sums.astype(jnp.bfloat16)
    far_part = couple(leaf_coef, couplings, distant_interaction_list)
    coarse_part = couple(parent_coef, coarse_couplings, coarse_list)
    down_part = jnp.repeat(coarse_part, BRANCH, axis=0)
    far_field = far_part + jnp.einsum("iab,ibp->iap", transfer_wide, down_part, precision=lax.Precision.HIGHEST)
    partial_field_output = far_field.astype(jnp.bfloat16)
    distant_block_rows = jnp.einsum("zmc,zmb->bzc", broad_basis_matrix, partial_field_output.astype(jnp.float32), precision=lax.Precision.HIGHEST)
    return (near_part + distant_block_rows).astype(jnp.bfloat16)


def reference(probes, near_blocks, leaf_cluster_basis, transfer, couplings, coarse_couplings, near_list, distant_interaction_list, coarse_list):
    first_apply = apply_once(probes, near_blocks, leaf_cluster_basis, transfer, couplings, coarse_couplings, near_list, distant_interaction_list, coarse_list)
    second_apply = apply_once(first_apply, near_blocks, leaf_cluster_basis, transfer, couplings, coarse_couplings, near_list, distant_interaction_list, coarse_list)
    return (first_apply, second_apply)
```

```python
import jax
import jax.numpy as jnp
from jax import lax
from jax.sharding import PartitionSpec as P

RANK = 64
BRANCH = 4
REACH = 4
CAP = 2


def from_sub(x):
    count = lax.axis_size("sub")
    return [
        lax.ppermute(x, "sub", [((i + k) % count, i) for i in range(count)]) for k in range(1, count)
    ]


def gather_sub(x):
    pieces = jnp.stack([x] + from_sub(x))
    return jnp.roll(pieces, lax.axis_index("sub"), axis=0)


def halo(x, width):
    count = lax.axis_size("leaf")
    low = lax.ppermute(x[-width:], "leaf", [(i, i + 1) for i in range(count - 1)])
    high = lax.ppermute(x[:width], "leaf", [(i + 1, i) for i in range(count - 1)])
    return jnp.concatenate([low, x, high], axis=0)


def local(
    probes,
    near_blocks,
    leaf_cluster_basis,
    transfer,
    couplings,
    coarse_couplings,
    near_list,
    distant_interaction_list,
    coarse_list,
):
    probe_count, leaf_dev, rows = probes.shape
    parent_dev = leaf_dev // BRANCH
    groups = lax.axis_size("leaf")
    subs = lax.axis_size("sub")
    sub = lax.axis_index("sub")
    first_leaf = lax.axis_index("leaf") * leaf_dev
    band = RANK // subs
    width = band * probe_count
    bf16, f32 = jnp.bfloat16, jnp.float32

    named = distant_interaction_list.reshape(-1)
    owner = jnp.where(named >= 0, named // leaf_dev, -1)
    place = named % leaf_dev
    of_peer = owner[None, :] == jnp.arange(groups)[:, None]
    least = jnp.min(jnp.where(of_peer, place[None, :], leaf_dev), axis=1)
    greatest = jnp.max(jnp.where(of_peer, place[None, :], -1), axis=1)
    asked = lax.all_to_all(jnp.stack([least, greatest], axis=1), "leaf", 0, 0, tiled=True)
    send_leaf = (asked.reshape(-1)[:, None] == jnp.arange(leaf_dev)[None, :]).astype(bf16)
    is_least = jnp.where(of_peer, place[None, :] == least[:, None], False)
    is_greatest = of_peer & ~is_least
    take_leaf = jnp.stack([is_least, is_greatest], axis=1).reshape(CAP * groups, -1).T.astype(bf16)
    take_parent = (
        coarse_list.reshape(-1)[:, None] == jnp.arange(groups * parent_dev)[None, :]
    ).astype(bf16)

    far_weights = lax.dynamic_slice_in_dim(couplings, sub * band, band, 3)
    coarse_weights = lax.dynamic_slice_in_dim(coarse_couplings, sub * band, band, 3)
    near_index = jnp.where(near_list >= 0, near_list - first_leaf + REACH, -1)
    near_take = (
        near_index.reshape(-1)[:, None] == jnp.arange(leaf_dev + 2 * REACH)[None, :]
    ).astype(bf16)

    basis_parts = gather_sub(leaf_cluster_basis.reshape(-1, 128))
    basis = basis_parts.reshape(subs, leaf_dev, RANK, rows).transpose(1, 2, 0, 3)
    basis = basis.reshape(leaf_dev, RANK, subs * rows)

    def whole(x):
        parts = gather_sub(x.reshape(-1, 128)).reshape(subs, leaf_dev, probe_count, rows)
        return parts.transpose(1, 2, 0, 3).reshape(leaf_dev, probe_count, subs * rows)

    def near(x):
        extended = halo(x.reshape(leaf_dev, -1), REACH)
        chosen = jnp.dot(near_take, extended, preferred_element_type=f32).astype(bf16)
        chosen = chosen.reshape(leaf_dev, near_list.shape[1], probe_count, subs * rows)
        return jnp.einsum("ikpc,ikrc->ipr", chosen, near_blocks, preferred_element_type=f32)

    def far(x):
        leaf_sums = jnp.einsum("iac,ipc->iap", basis, x, preferred_element_type=f32)
        leaf_coef = leaf_sums.astype(bf16)
        parent_sums = jnp.einsum("iab,iap->ibp", transfer, leaf_coef, preferred_element_type=f32)
        parent_coef = parent_sums.reshape(parent_dev, BRANCH, RANK, probe_count).sum(1).astype(bf16)
        leaf_band = lax.dynamic_slice_in_dim(leaf_coef, sub * band, band, 1).reshape(leaf_dev, width)
        parent_band = lax.dynamic_slice_in_dim(parent_coef, sub * band, band, 1)
        parent_band = parent_band.reshape(1, parent_dev, width)
        leaf_out = jnp.dot(send_leaf, leaf_band, preferred_element_type=f32).astype(bf16)
        out = jnp.concatenate(
            [
                leaf_out.reshape(groups, CAP, width),
                jnp.broadcast_to(parent_band, (groups, parent_dev, width)),
            ],
            axis=1,
        )
        got = lax.all_to_all(out, "leaf", 0, 0, tiled=True)
        got_leaf = got[:, :CAP].reshape(groups * CAP, width)
        got_parent = got[:, CAP:].reshape(groups * parent_dev, width)
        picked = jnp.dot(take_leaf, got_leaf, preferred_element_type=f32).astype(bf16)
        picked = picked.reshape(leaf_dev, -1, band, probe_count)
        coarse_picked = jnp.dot(take_parent, got_parent, preferred_element_type=f32).astype(bf16)
        coarse_picked = coarse_picked.reshape(parent_dev, -1, band, probe_count)
        far_part = jnp.einsum("ikab,ikbp->iap", far_weights, picked, preferred_element_type=f32)
        coarse_part = jnp.einsum(
            "qkab,qkbp->qap", coarse_weights, coarse_picked, preferred_element_type=f32
        )
        down = jnp.repeat(coarse_part.astype(bf16), BRANCH, axis=0)
        far_part = far_part + jnp.einsum("iab,ibp->iap", transfer, down, preferred_element_type=f32)
        flat = far_part.reshape(leaf_dev, -1)
        others = from_sub(flat.astype(bf16))
        total = flat + sum(piece.astype(f32) for piece in others)
        return total.astype(bf16).reshape(leaf_dev, RANK, probe_count)

    def spread(field, some_basis):
        return jnp.einsum("iar,iap->ipr", some_basis, field, preferred_element_type=f32)

    x0 = whole(probes.transpose(1, 0, 2))
    near1 = near(x0)
    near1_whole = whole(near1.astype(bf16))
    field1 = far(x0)
    first = (near1 + spread(field1, leaf_cluster_basis)).astype(bf16)
    x1 = (near1_whole.astype(f32) + spread(field1, basis)).astype(bf16)
    near2 = near(x1)
    field2 = far(x1)
    second = (near2 + spread(field2, leaf_cluster_basis)).astype(bf16)
    return (first.transpose(1, 0, 2), second.transpose(1, 0, 2))


def solution(mesh):
    return jax.shard_map(
        local,
        mesh=mesh,
        in_specs=(
            P(None, "leaf", "sub"),
            P("leaf", None, "sub", None),
            P("leaf", None, "sub"),
            P("leaf", None, None),
            P("leaf", None, None, None),
            P("leaf", None, None, None),
            P("leaf", None),
            P("leaf", None),
            P("leaf", None),
        ),
        out_specs=(P(None, "leaf", "sub"), P(None, "leaf", "sub")),
        check_vma=False,
    )
```

```python
import jax
import jax.numpy as jnp
from jax import lax
from jax.experimental import pallas as pl
from jax.experimental.pallas import tpu as pltpu
from jax.sharding import PartitionSpec as P

RANK = 64
BRANCH = 4
REACH = 4
CAP = 2
LEAVES = 16
PARENTS = 4
PROBES = 32
ROWS = 64
SUBS = 4
UNKNOWNS = SUBS * ROWS
BAND = RANK // SUBS
NEAR = 9
FAR = 16
PLANES = 8
PLANE = 8
TILES = (LEAVES + PARENTS) // 4
OUT_TILES = PLANES * CAP // 4 + PLANES
BF16, F32 = jnp.bfloat16, jnp.float32

NT = (((1,), (1,)), ((), ()))
VMEM_LIMIT = 24 * 1024 * 1024


def dot(x, y):
    return jnp.dot(x, y, preferred_element_type=F32)


def dot_nt(x, y):
    return lax.dot_general(x, y, NT, preferred_element_type=F32)


def call(kernel, name, outs, args, smem, scratch=()):
    in_specs = [pl.BlockSpec(memory_space=pltpu.SMEM)] * smem
    in_specs += [pl.BlockSpec(memory_space=pltpu.VMEM)] * (len(args) - smem)
    return pl.pallas_call(
        kernel,
        name=name,
        out_shape=[jax.ShapeDtypeStruct(s, d) for s, d in outs],
        in_specs=in_specs,
        out_specs=[pl.BlockSpec(memory_space=pltpu.VMEM)] * len(outs),
        scratch_shapes=list(scratch),
        compiler_params=pltpu.CompilerParams(vmem_limit_bytes=VMEM_LIMIT),
    )(*args)


def pack_kernel(x_ref, basis_ref, out_ref):
    x = jnp.transpose(x_ref[...].astype(F32), (1, 0, 2)).astype(BF16)
    for j in range(LEAVES // 2):
        pair = jnp.concatenate([x[2 * j], x[2 * j + 1]], axis=1)
        basis = jnp.concatenate([basis_ref[2 * j], basis_ref[2 * j + 1]], axis=1)
        for s in range(SUBS):
            out_ref[s, pl.ds(j * PROBES, PROBES), :] = pair
            out_ref[s, pl.ds(LEAVES // 2 * PROBES + j * RANK, RANK), :] = basis


def unpack(ref, i, start, rows):
    half = slice((i % 2) * ROWS, (i % 2 + 1) * ROWS)
    place = pl.ds(start + (i // 2) * rows, rows)
    return jnp.concatenate([ref[s, place, half] for s in range(SUBS)], axis=1)


def coefficients(sub_ref, leaf_x, leaf_basis, transfer_t_ref, out_ref, band_ref):
    band = pl.ds(pl.multiple_of(sub_ref[0] * BAND, BAND), BAND)
    parents = []
    for q in range(PARENTS):
        sums = [dot_nt(leaf_basis(i), leaf_x(i)) for i in range(4 * q, 4 * q + 4)]
        band_ref[q] = jnp.concatenate(sums, axis=1)
        tall = jnp.concatenate([s.astype(BF16) for s in sums], axis=0)
        parents.append(dot(transfer_t_ref[q], tall))
    band_ref[PARENTS] = jnp.concatenate(parents, axis=1)
    for t in range(TILES):
        tile = band_ref[t, band, :].astype(BF16)
        for z in range(PLANES):
            out_ref[z, t] = tile


def first_kernel(sub_ref, got_ref, transfer_t_ref, x_ref, basis_ref, low_ref, high_ref, out_ref, band_ref):
    for i in range(LEAVES):
        x = unpack(got_ref, i, 0, PROBES)
        x_ref[i] = x
        if i < REACH:
            low_ref[i] = x
        if i >= LEAVES - REACH:
            high_ref[i - (LEAVES - REACH)] = x
        basis_ref[i] = unpack(got_ref, i, LEAVES // 2 * PROBES, RANK)
    coefficients(
        sub_ref, lambda i: x_ref[i], lambda i: basis_ref[i], transfer_t_ref, out_ref, band_ref
    )


def field_of(got_ref, q):
    total = got_ref[0, q].astype(F32)
    for s in range(1, SUBS):
        total = total + got_ref[s, q].astype(F32)
    return jnp.transpose(total).astype(BF16)


def second_kernel(
    sub_ref, field_ref, near_ref, basis_ref, transfer_t_ref, x_ref, low_ref, high_ref, out_ref, band_ref
):
    for q in range(PARENTS):
        field = field_of(field_ref, q)
        for c in range(4):
            i = 4 * q + c
            far = dot(field[c * PROBES : (c + 1) * PROBES], basis_ref[i])
            x = (unpack(near_ref, i, 0, PROBES).astype(F32) + far).astype(BF16)
            x_ref[i] = x
            if i < REACH:
                low_ref[i] = x
            if i >= LEAVES - REACH:
                high_ref[i - (LEAVES - REACH)] = x
    coefficients(
        sub_ref, lambda i: x_ref[i], lambda i: basis_ref[i], transfer_t_ref, out_ref, band_ref
    )


def output_kernel(field_ref, near_ref, basis_ref, out_ref):
    outs = []
    for q in range(PARENTS):
        field = field_of(field_ref, q)
        for c in range(4):
            i = 4 * q + c
            outs.append(near_ref[i] + dot(field[c * PROBES : (c + 1) * PROBES], basis_ref[i]))
    out_ref[...] = jnp.transpose(jnp.stack(outs), (1, 0, 2)).astype(BF16)


def near_kernel(index_ref, x_ref, low_ref, high_ref, blocks_ref, out_ref, packed_ref, wide_ref):
    wide_ref[pl.ds(0, REACH)] = low_ref[...]
    wide_ref[pl.ds(REACH, LEAVES)] = x_ref[...]
    wide_ref[pl.ds(REACH + LEAVES, REACH)] = high_ref[...]
    wide_ref[2 * REACH + LEAVES] = jnp.zeros((PROBES, UNKNOWNS), BF16)
    for j in range(LEAVES // 2):
        pair = []
        for i in (2 * j, 2 * j + 1):
            total = jnp.zeros((PROBES, ROWS), F32)
            for k in range(NEAR):
                total = total + dot_nt(wide_ref[index_ref[i * NEAR + k]], blocks_ref[i, k])
            out_ref[i] = total
            pair.append(total.astype(BF16))
        both = jnp.concatenate(pair, axis=1)
        for s in range(SUBS):
            packed_ref[s, pl.ds(j * PROBES, PROBES), :] = both


def quarter_lanes():
    return lax.broadcasted_iota(jnp.int32, (BAND, 4 * PROBES), 1) // PROBES


def choose_kernel(asked_ref, got_ref, out_ref, rows_ref):
    for z in range(PLANES):
        for i in range(LEAVES):
            c = i % 4
            piece = got_ref[z, i // 4][:, c * PROBES : (c + 1) * PROBES]
            rows_ref[z * LEAVES + i] = jnp.concatenate([piece] * 4, axis=1)
    quarter = quarter_lanes()
    for m in range(PLANE):
        for t in range(PLANES * CAP // 4):
            tile = None
            for c in range(4):
                n = 4 * t + c
                row = rows_ref[n // CAP * LEAVES + asked_ref[m * PLANES * CAP + n]]
                tile = row if tile is None else jnp.where(quarter == c, row, tile)
            out_ref[m, t] = tile
        for z in range(PLANES):
            out_ref[m, PLANES * CAP // 4 + z] = got_ref[z, TILES - 1]


def fold(x):
    x = x + pltpu.roll(x, 2 * PROBES, 1)
    return x + pltpu.roll(x, PROBES, 1)


def far_kernel(far_ref, coarse_ref, got_ref, weights_ref, coarse_weights_ref, transfer_ref, out_ref):
    quarter = quarter_lanes()
    zero = jnp.zeros((BAND, 4 * PROBES), BF16)

    def picked(index_ref, first):
        tiles = []
        for k in range(FAR):
            index = index_ref[first + k]
            tiles.append(jnp.where(quarter == index % 8, got_ref[index // 8], zero))
        return jnp.concatenate(tiles, axis=0)

    wide_quarter = lax.broadcasted_iota(jnp.int32, (RANK, 4 * PROBES), 1) // PROBES
    for q in range(PARENTS):
        coarse = fold(dot(coarse_weights_ref[q], picked(coarse_ref, q * FAR))).astype(BF16)
        down = dot(transfer_ref[q], coarse)
        total = None
        for c in range(4):
            i = 4 * q + c
            part = fold(dot(weights_ref[i], picked(far_ref, i * FAR)))
            part = part + down[c * RANK : (c + 1) * RANK]
            total = part if total is None else jnp.where(wide_quarter == c, part, total)
        for s in range(SUBS):
            out_ref[s, q] = total.astype(BF16)


def weights_kernel(sub_ref, couplings_ref, coarse_ref, out_ref, coarse_out_ref, move_ref):
    source = lax.broadcasted_iota(jnp.int32, (RANK, FAR * BAND), 0) - sub_ref[0] * BAND
    target = lax.broadcasted_iota(jnp.int32, (RANK, FAR * BAND), 1)
    inside = (source >= 0) & (source < BAND)
    for k in range(FAR):
        hit = inside & (target == source + k * BAND)
        move_ref[k] = jnp.where(hit, 1.0, 0.0).astype(BF16)

    def reorder(from_ref, to_ref):
        def body(i, carry):
            total = dot(from_ref[i, 0], move_ref[0])
            for k in range(1, FAR):
                total = total + dot(from_ref[i, k], move_ref[k])
            to_ref[i] = total.astype(BF16)
            return carry

        lax.fori_loop(0, from_ref.shape[0], body, 0)

    reorder(couplings_ref, out_ref)
    reorder(coarse_ref, coarse_out_ref)


def local(
    probes,
    near_blocks,
    leaf_cluster_basis,
    transfer,
    couplings,
    coarse_couplings,
    near_list,
    distant_interaction_list,
    coarse_list,
):
    groups = PLANES * PLANE
    in_plane = [[z * PLANE + m for m in range(PLANE)] for z in range(PLANES)]
    along_z = [[z * PLANE + m for z in range(PLANES)] for m in range(PLANE)]
    sub = lax.axis_index("sub").reshape(1)
    first_leaf = lax.axis_index("leaf") * LEAVES

    named = distant_interaction_list.reshape(-1)
    owner = jnp.where(named >= 0, named // LEAVES, -1)
    place = named % LEAVES
    of_peer = owner[None, :] == jnp.arange(groups)[:, None]
    least = jnp.min(jnp.where(of_peer, place[None, :], LEAVES - 1), axis=1)
    greatest = jnp.max(jnp.where(of_peer, place[None, :], 0), axis=1)
    wanted = jnp.stack([least, greatest], axis=1).reshape(PLANES, PLANE, CAP)
    wanted = wanted.transpose(1, 0, 2).reshape(PLANE, PLANES * CAP)
    asked = lax.all_to_all(wanted, "leaf", 0, 0, axis_index_groups=in_plane, tiled=True)
    asked = asked.reshape(-1)

    def address(live, row, group):
        row = row + (group % PLANE) * OUT_TILES * 4
        return jnp.where(live, row // 4 * 8 + row % 4, 4)

    least_named = jnp.max(jnp.where(of_peer, least[:, None], 0), axis=0)
    second = (place != least_named).astype(jnp.int32)
    far_index = address(named >= 0, owner // PLANE * CAP + second, owner)
    coarse = coarse_list.reshape(-1)
    coarse_owner = coarse // PARENTS
    coarse_index = address(
        coarse >= 0,
        PLANES * CAP + coarse_owner // PLANE * PARENTS + coarse % PARENTS,
        coarse_owner,
    )
    near_index = near_list.reshape(-1)
    near_index = jnp.where(near_index >= 0, near_index - first_leaf + REACH, LEAVES + 2 * REACH)

    transfer_down = transfer.reshape(PARENTS, BRANCH * RANK, RANK)
    transfer_up = jnp.swapaxes(transfer_down, 1, 2)

    weights, coarse_weights = call(
        weights_kernel,
        "order_couplings",
        [((LEAVES, RANK, FAR * BAND), BF16), ((PARENTS, RANK, FAR * BAND), BF16)],
        [sub, couplings, coarse_couplings],
        1,
        [pltpu.VMEM((FAR, RANK, FAR * BAND), BF16)],
    )

    def over_sub(x):
        return lax.all_to_all(x, "sub", 0, 0, tiled=True)

    x_shape = (LEAVES, PROBES, UNKNOWNS)
    edge = (REACH, PROBES, UNKNOWNS)
    message = (PLANES, TILES, BAND, 4 * PROBES)
    packed_rows = LEAVES // 2 * PROBES
    band_scratch = [pltpu.VMEM((TILES, RANK, 4 * PROBES), F32)]

    def exchange(tiles):
        column = lax.all_to_all(tiles, "leaf", 0, 0, axis_index_groups=along_z, tiled=True)
        (chosen,) = call(
            choose_kernel,
            "choose_rows",
            [((PLANE, OUT_TILES, BAND, 4 * PROBES), BF16)],
            [asked, column],
            1,
            [pltpu.VMEM((PLANES * LEAVES, BAND, 4 * PROBES), BF16)],
        )
        got = lax.all_to_all(chosen, "leaf", 0, 0, axis_index_groups=in_plane, tiled=True)
        return got.reshape(PLANE * OUT_TILES, BAND, 4 * PROBES)

    def far(tiles):
        (part,) = call(
            far_kernel,
            "far_field",
            [((SUBS, PARENTS, RANK, 4 * PROBES), BF16)],
            [far_index, coarse_index, exchange(tiles), weights, coarse_weights, transfer_down],
            2,
        )
        return over_sub(part)

    def near(x, low, high):
        count = groups
        from_below = lax.ppermute(high, "leaf", [(i, i + 1) for i in range(count - 1)])
        from_above = lax.ppermute(low, "leaf", [(i + 1, i) for i in range(count - 1)])
        return call(
            near_kernel,
            "near_field",
            [((LEAVES, PROBES, ROWS), F32), ((SUBS, packed_rows, 2 * ROWS), BF16)],
            [near_index, x, from_below, from_above, near_blocks],
            1,
            [pltpu.VMEM((LEAVES + 2 * REACH + 1, PROBES, UNKNOWNS), BF16)],
        )

    def output(field, near_part):
        return call(
            output_kernel,
            "output",
            [((PROBES, LEAVES, ROWS), BF16)],
            [field, near_part, leaf_cluster_basis],
            0,
        )[0]

    (packed,) = call(
        pack_kernel,
        "pack",
        [((SUBS, packed_rows + LEAVES // 2 * RANK, 2 * ROWS), BF16)],
        [probes, leaf_cluster_basis],
        0,
    )
    x0, basis, low, high, tiles = call(
        first_kernel,
        "first_coefficients",
        [
            (x_shape, BF16),
            ((LEAVES, RANK, UNKNOWNS), BF16),
            (edge, BF16),
            (edge, BF16),
            (message, BF16),
        ],
        [sub, over_sub(packed), transfer_up],
        1,
        band_scratch,
    )
    near1, near1_packed = near(x0, low, high)
    near1_whole = over_sub(near1_packed)
    field1 = far(tiles)
    x1, low, high, tiles = call(
        second_kernel,
        "second_coefficients",
        [(x_shape, BF16), (edge, BF16), (edge, BF16), (message, BF16)],
        [sub, field1, near1_whole, basis, transfer_up],
        1,
        band_scratch,
    )
    first = output(field1, near1)
    near2, _ = near(x1, low, high)
    field2 = far(tiles)
    return (first, output(field2, near2))


def solution(mesh):
    return jax.shard_map(
        local,
        mesh=mesh,
        in_specs=(
            P(None, "leaf", "sub"),
            P("leaf", None, "sub", None),
            P("leaf", None, "sub"),
            P("leaf", None, None),
            P("leaf", None, None, None),
            P("leaf", None, None, None),
            P("leaf", None),
            P("leaf", None),
            P("leaf", None),
        ),
        out_specs=(P(None, "leaf", "sub"), P(None, "leaf", "sub")),
        check_vma=False,
    )
```

```python
import jax
import jax.numpy as jnp
from jax import lax
from jax.experimental import pallas as pl
from jax.experimental.pallas import tpu as pltpu
from jax.sharding import PartitionSpec as P

RANK = 64
BRANCH = 4
REACH = 4
CAP = 2
LEAVES = 16
PARENTS = 4
PROBES = 32
ROWS = 64
SUBS = 4
OWN = PROBES // SUBS
UNKNOWNS = SUBS * ROWS
NEAR = 9
FAR = 16
PLANES = 8
PLANE = 8
LANES = 128
TILES = PARENTS + 1
LEAF_OUT = PLANES * CAP // 4
OUT_TILES = LEAF_OUT + PLANES
GOT_ROWS = 4 * PLANE * OUT_TILES
PACKED = LEAVES // 2 * PROBES
SENT = 16 * PARENTS + LEAVES // 2 * RANK
BF16, F32 = jnp.bfloat16, jnp.float32

NT = (((1,), (1,)), ((), ()))
VMEM_LIMIT = 16 * 1024 * 1024


def dot(x, y):
    return jnp.dot(x, y, preferred_element_type=F32)


def dot_nt(x, y):
    return lax.dot_general(x, y, NT, preferred_element_type=F32)


def call(kernel, name, outs, args, scratch=(), chunks=1):
    spaces = {"smem": pltpu.SMEM, "vmem": pltpu.VMEM, "hbm": pltpu.HBM, "cut": pltpu.HBM, "any": pl.ANY}
    moved = [j for j, (kind, _) in enumerate(args) if kind in ("hbm", "any", "cut")]
    buffers = [pltpu.VMEM(args[j][1].shape, args[j][1].dtype) for j in moved]
    scratch = list(scratch)

    def body(*refs):
        refs = list(refs)
        sems = refs.pop()
        front = len(args) + len(outs) + len(scratch)
        whole, parts = [], []
        for n, j in enumerate(moved):
            source, target = refs[j], refs[front + n]
            if args[j][0] == "cut":
                size = target.shape[0] // chunks
                for c in range(chunks):
                    part = pl.ds(c * size, size)
                    parts.append(
                        pltpu.make_async_copy(source.at[part], target.at[part], sems.at[len(moved) + c])
                    )
            else:
                whole.append(pltpu.make_async_copy(source, target, sems.at[n]))
            refs[j] = target
        for copy in whole + parts:
            copy.start()
        for copy in whole:
            copy.wait()
        extra = [lambda c: parts[c].wait()] if parts else []
        kernel(*refs[:front], *extra)

    return pl.pallas_call(
        body,
        name=name,
        out_shape=[jax.ShapeDtypeStruct(s, d) for s, d in outs],
        in_specs=[pl.BlockSpec(memory_space=spaces[kind]) for kind, _ in args],
        out_specs=[pl.BlockSpec(memory_space=pltpu.VMEM)] * len(outs),
        scratch_shapes=scratch + buffers + [pltpu.SemaphoreType.DMA((len(moved) + chunks,))],
        compiler_params=pltpu.CompilerParams(vmem_limit_bytes=VMEM_LIMIT),
    )(*[
        pltpu.with_memory_space_constraint(array, pltpu.HBM) if kind in ("hbm", "cut") else array
        for kind, array in args
    ])


def of_kind(kind, *arrays):
    return [(kind, array) for array in arrays]


def lane_block(rows, lanes):
    return lax.broadcasted_iota(jnp.int32, (rows, lanes), 1) // RANK


def diagonal(x, rows):
    block = lane_block(rows, 4 * RANK)
    out = x[:rows]
    for c in range(1, 4):
        out = jnp.where(block == c, x[c * rows : (c + 1) * rows], out)
    return out


def spread_diagonal(x):
    block = lane_block(x.shape[0], 4 * RANK)
    return jnp.concatenate([jnp.where(block == c, x, jnp.zeros_like(x)) for c in range(4)], axis=0)


def to_tile(x):
    return jnp.concatenate([x[:, :LANES], x[:, LANES:]], axis=0).astype(BF16)


def tile_row(tile, c):
    h, g = c // 2, c % 2
    return tile[h * OWN : (h + 1) * OWN, g * RANK : (g + 1) * RANK]


def index_kernel(
    first_ref, far_ref, coarse_ref, near_ref, wanted_ref, far_out_ref, coarse_out_ref, near_out_ref
):
    groups = PLANES * PLANE
    group = lax.broadcasted_iota(jnp.int32, (groups, FAR), 0)
    named = far_ref[...]
    owner = jnp.where(named >= 0, named >> 4, -1)
    place = (named & (LEAVES - 1)).astype(F32)
    hits = [owner[i : i + 1] == group for i in range(LEAVES)]
    least = jnp.full((groups, FAR), LEAVES - 1.0, F32)
    greatest = jnp.zeros((groups, FAR), F32)
    for i in range(LEAVES):
        least = jnp.minimum(least, jnp.where(hits[i], place[i : i + 1], LEAVES - 1.0))
        greatest = jnp.maximum(greatest, jnp.where(hits[i], place[i : i + 1], 0.0))
    least = jnp.min(least, axis=1, keepdims=True)
    greatest = jnp.max(greatest, axis=1, keepdims=True)
    lane = lax.broadcasted_iota(jnp.int32, (PLANE, LANES), 1)
    wanted = jnp.zeros((PLANE, LANES), F32)
    for z in range(PLANES):
        wanted = jnp.where(lane == CAP * z, least[z * PLANE : (z + 1) * PLANE], wanted)
        wanted = jnp.where(lane == CAP * z + 1, greatest[z * PLANE : (z + 1) * PLANE], wanted)
    wanted_ref[...] = wanted.astype(jnp.int32)
    of_entry = [
        jnp.sum(jnp.where(hits[i], least, 0.0), axis=0, keepdims=True) for i in range(LEAVES)
    ]
    second = jnp.where(place == jnp.concatenate(of_entry, axis=0), 0, 1)
    row = (owner & (PLANE - 1)) * (4 * OUT_TILES) + (owner >> 3) * CAP + second
    far_out_ref[...] = jnp.where(named >= 0, row, GOT_ROWS)
    coarse = coarse_ref[...]
    owner = coarse >> 2
    row = (owner & (PLANE - 1)) * (4 * OUT_TILES) + 4 * LEAF_OUT + (owner >> 3) * PARENTS
    coarse_out_ref[...] = jnp.where(coarse >= 0, row + (coarse & (PARENTS - 1)), GOT_ROWS)
    near = near_ref[...]
    near_out_ref[...] = jnp.where(near >= 0, near - first_ref[0] + REACH, LEAVES + 2 * REACH)


def partial_kernel(
    sub_ref, x_ref, basis_ref, transfer_ref, out0_ref, out1_ref, out2_ref, out3_ref, sums_ref
):
    out_refs = [out0_ref, out1_ref, out2_ref, out3_ref]
    x = jnp.transpose(x_ref[...].astype(F32), (1, 0, 2)).astype(BF16)
    for j in range(LEAVES // 2):
        pair = jnp.concatenate([x[2 * j], x[2 * j + 1]], axis=1)
        for out_ref in out_refs:
            out_ref[pl.ds(j * PROBES, PROBES), :] = pair
    parents = []
    sums = []
    for q in range(PARENTS):
        four = x[4 * q : 4 * q + 4].reshape(4 * PROBES, ROWS)
        leaf = diagonal(dot_nt(four, basis_ref[q]), PROBES)
        sums.append(leaf)
        parents.append(dot(leaf.astype(BF16), transfer_ref[q]))
    sums.append(jnp.concatenate(parents, axis=1))
    for t in range(TILES):
        sums_ref[t] = sums[t]
    for k, out_ref in enumerate(out_refs):
        place = probes_of((sub_ref[0] + k) % SUBS)
        for t in range(TILES):
            out_ref[pl.ds(PACKED + 16 * t, 16), :] = to_tile(sums_ref[t, place, :])


def probes_of(sub):
    return pl.ds(pl.multiple_of(sub * OWN, OWN), OWN)


def in_order(sub_ref, piece_refs, slots_ref, rows):
    for k, piece_ref in enumerate(piece_refs):
        slots_ref[(sub_ref[0] + SUBS - k) % SUBS] = piece_ref[:rows]


def first_kernel(
    sub_ref, got0_ref, got1_ref, got2_ref, got3_ref, x_ref, low_ref, high_ref, out_ref, slots_ref
):
    got_refs = [got0_ref, got1_ref, got2_ref, got3_ref]
    for t in range(TILES):
        total = got0_ref[pl.ds(PACKED + 16 * t, 16), :].astype(F32)
        for got_ref in got_refs[1:]:
            total = total + got_ref[pl.ds(PACKED + 16 * t, 16), :].astype(F32)
        tile = total.astype(BF16)
        for z in range(PLANES):
            out_ref[z, t] = tile
    in_order(sub_ref, got_refs, slots_ref, PACKED)
    for i in range(LEAVES):
        half = slice((i % 2) * ROWS, (i % 2 + 1) * ROWS)
        rows = pl.ds((i // 2) * PROBES, PROBES)
        x = jnp.concatenate([slots_ref[s, rows, half] for s in range(SUBS)], axis=1)
        x_ref[i] = x
        if i < REACH:
            low_ref[i] = x
        if i >= LEAVES - REACH:
            high_ref[i - (LEAVES - REACH)] = x


def join_kernel(sub_ref, got0_ref, got1_ref, got2_ref, got3_ref, near_ref, basis_ref, slots_ref):
    in_order(sub_ref, [got0_ref, got1_ref, got2_ref, got3_ref], slots_ref, SENT)
    for q in range(PARENTS):
        tiles = [slots_ref[s, pl.ds(16 * q, 16), :].astype(F32) for s in range(SUBS)]
        near = [jnp.concatenate([tile_row(t, c) for t in tiles], axis=1) for c in range(4)]
        near_ref[q] = jnp.concatenate(near, axis=0).astype(BF16)
    for i in range(LEAVES):
        half = slice((i % 2) * ROWS, (i % 2 + 1) * ROWS)
        rows = pl.ds(16 * PARENTS + (i // 2) * RANK, RANK)
        whole = jnp.concatenate([slots_ref[s, rows, half] for s in range(SUBS)], axis=1)
        basis_ref[i // 4, pl.ds(i % 4 * RANK, RANK), :] = whole


def weights_kernel(_, couplings_ref, coarse_ref, out_ref):
    for q in range(PARENTS + 1):
        for c in range(4):
            for k in range(0, FAR, 2):
                if q < PARENTS:
                    pair = [couplings_ref[4 * q + c, k], couplings_ref[4 * q + c, k + 1]]
                else:
                    pair = [coarse_ref[c, k], coarse_ref[c, k + 1]]
                both = jnp.concatenate(pair, axis=1)
                out_ref[q, pl.ds(c * RANK, RANK), pl.ds(k * RANK, LANES)] = both


def both_halves(row_pair):
    turned = pltpu.roll(row_pair, RANK, 1)
    left = lax.broadcasted_iota(jnp.int32, row_pair.shape, 1) < RANK
    return jnp.where(left, row_pair, turned), jnp.where(left, turned, row_pair)


def unpack_tile(tile, rows_ref, first):
    wide = tile.astype(F32)
    for h in range(2):
        one, two = both_halves(wide[h * OWN : (h + 1) * OWN])
        rows_ref[first + 2 * h] = one
        rows_ref[first + 2 * h + 1] = two


def choose_kernel(asked_ref, got_ref, out_ref, rows_ref):
    for z in range(PLANES):
        for t in range(LEAVES // 4):
            unpack_tile(got_ref[z, t], rows_ref, z * LEAVES + 4 * t)
    left = lax.broadcasted_iota(jnp.int32, (OWN, LANES), 1) < RANK
    for m in range(PLANE):
        for t in range(LEAF_OUT):
            rows = []
            for n in range(4 * t, 4 * t + 4):
                rows.append(rows_ref[n // CAP * LEAVES + asked_ref[m, n]])
            top = jnp.where(left, rows[0], rows[1])
            bottom = jnp.where(left, rows[2], rows[3])
            out_ref[m, t] = jnp.concatenate([top, bottom], axis=0).astype(BF16)
        for z in range(PLANES):
            out_ref[m, LEAF_OUT + z] = got_ref[z, TILES - 1]


def far_field(far_ref, coarse_ref, got_ref, weights_ref, transfer_ref, rows_ref):
    for n in range(PLANE * OUT_TILES):
        unpack_tile(got_ref[n], rows_ref, 4 * n)
    rows_ref[GOT_ROWS] = jnp.zeros((OWN, LANES), F32)
    left = lax.broadcasted_iota(jnp.int32, (OWN, LANES), 1) < RANK

    def apply(index_ref, q, weights):
        picked = []
        for c in range(4):
            pairs = []
            for k in range(0, FAR, 2):
                one = rows_ref[index_ref[4 * q + c, k]]
                two = rows_ref[index_ref[4 * q + c, k + 1]]
                pairs.append(jnp.where(left, one, two))
            picked.append(jnp.concatenate(pairs, axis=1))
        picked = jnp.concatenate(picked, axis=0).astype(BF16)
        return diagonal(dot_nt(picked, weights), OWN)

    coarse = apply(coarse_ref, 0, weights_ref[PARENTS]).astype(BF16)
    fields = []
    for q in range(PARENTS):
        down = dot_nt(coarse[:, q * RANK : (q + 1) * RANK], transfer_ref[q])
        fields.append(apply(far_ref, q, weights_ref[q]) + down)
    return fields


def middle_kernel(
    far_ref,
    coarse_ref,
    got_ref,
    weights_ref,
    transfer_ref,
    basis_ref,
    near_ref,
    x_ref,
    out_ref,
    rows_ref,
):
    fields = far_field(far_ref, coarse_ref, got_ref, weights_ref, transfer_ref, rows_ref)
    tiles = []
    parents = []
    for q in range(PARENTS):
        far = dot(spread_diagonal(fields[q]).astype(BF16), basis_ref[q])
        x = (near_ref[q].astype(F32) + far).astype(BF16)
        x_ref[q] = x
        leaf = diagonal(dot_nt(x, basis_ref[q]), OWN)
        tiles.append(to_tile(leaf))
        parents.append(dot(leaf.astype(BF16), transfer_ref[q]))
    tiles.append(to_tile(jnp.concatenate(parents, axis=1)))
    for t in range(TILES):
        for z in range(PLANES):
            out_ref[z, t] = tiles[t]


def last_field_kernel(
    far_ref, coarse_ref, got_ref, weights_ref, transfer_ref, out_ref, rows_ref
):
    fields = far_field(far_ref, coarse_ref, got_ref, weights_ref, transfer_ref, rows_ref)
    for q in range(PARENTS):
        out_ref[q] = to_tile(fields[q])


def whole_kernel(
    sub_ref,
    got0_ref,
    got1_ref,
    got2_ref,
    got3_ref,
    x_ref,
    low_ref,
    high_ref,
    first_ref,
    got_ref,
):
    in_order(sub_ref, [got0_ref, got1_ref, got2_ref, got3_ref], got_ref, PARENTS)
    sub = sub_ref[0]
    outs = []
    for q in range(PARENTS):
        parts = [got_ref[s, q].astype(F32) for s in range(SUBS)]
        for c in range(4):
            i = 4 * q + c
            rows = slice(c * OWN, (c + 1) * OWN)
            wide = jnp.concatenate([part[rows] for part in parts], axis=0)
            x = wide.astype(BF16)
            x_ref[i] = x
            if i < REACH:
                low_ref[i] = x
            if i >= LEAVES - REACH:
                high_ref[i - (LEAVES - REACH)] = x
            mine = wide[:, :ROWS]
            for s in range(1, SUBS):
                mine = jnp.where(sub == s, wide[:, s * ROWS : (s + 1) * ROWS], mine)
            outs.append(mine)
    first_ref[...] = jnp.transpose(jnp.stack(outs), (1, 0, 2)).astype(BF16)


def output_kernel(
    sub_ref, field0_ref, field1_ref, field2_ref, field3_ref, near_ref, basis_ref, out_ref, field_ref
):
    in_order(sub_ref, [field0_ref, field1_ref, field2_ref, field3_ref], field_ref, PARENTS)
    outs = []
    for q in range(PARENTS):
        tiles = [field_ref[s, q].astype(F32) for s in range(SUBS)]
        field = jnp.concatenate(
            [jnp.concatenate([t[:OWN], t[OWN:]], axis=1) for t in tiles], axis=0
        )
        far = dot(spread_diagonal(field).astype(BF16), basis_ref[q])
        for c in range(4):
            outs.append(near_ref[4 * q + c] + far[c * PROBES : (c + 1) * PROBES])
    out_ref[...] = jnp.transpose(jnp.stack(outs), (1, 0, 2)).astype(BF16)


def near_parts(index_ref, x_ref, low_ref, high_ref, blocks_ref, wide_ref, arrived):
    wide_ref[pl.ds(0, REACH)] = low_ref[...]
    wide_ref[pl.ds(REACH, LEAVES)] = x_ref[...]
    wide_ref[pl.ds(REACH + LEAVES, REACH)] = high_ref[...]
    wide_ref[2 * REACH + LEAVES] = jnp.zeros((PROBES, UNKNOWNS), BF16)
    for q in range(PARENTS):
        arrived(q)
        four = []
        for i in range(4 * q, 4 * q + 4):
            total = jnp.zeros((PROBES, ROWS), F32)
            for k in range(NEAR):
                total = total + dot_nt(wide_ref[index_ref[i, k]], blocks_ref[i, k])
            four.append(total)
        yield four


def near_sent_kernel(
    sub_ref,
    index_ref,
    x_ref,
    low_ref,
    high_ref,
    blocks_ref,
    basis_ref,
    out0_ref,
    out1_ref,
    out2_ref,
    out3_ref,
    wide_ref,
    four_ref,
    arrived,
):
    out_refs = [out0_ref, out1_ref, out2_ref, out3_ref]
    for j in range(LEAVES // 2):
        pair = jnp.concatenate([basis_ref[2 * j], basis_ref[2 * j + 1]], axis=1)
        for out_ref in out_refs:
            out_ref[pl.ds(16 * PARENTS + j * RANK, RANK), :] = pair
    parts = near_parts(index_ref, x_ref, low_ref, high_ref, blocks_ref, wide_ref, arrived)
    for q, four in enumerate(parts):
        four_ref[...] = jnp.concatenate(four, axis=1)
        for k, out_ref in enumerate(out_refs):
            tile = to_tile(four_ref[probes_of((sub_ref[0] + k) % SUBS), :])
            out_ref[pl.ds(16 * q, 16), :] = tile


def near_kernel(index_ref, x_ref, low_ref, high_ref, blocks_ref, out_ref, wide_ref, arrived):
    parts = near_parts(index_ref, x_ref, low_ref, high_ref, blocks_ref, wide_ref, arrived)
    for q, four in enumerate(parts):
        for c in range(4):
            out_ref[4 * q + c] = four[c]


def local(
    probes,
    near_blocks,
    leaf_cluster_basis,
    transfer,
    couplings,
    coarse_couplings,
    near_list,
    distant_interaction_list,
    coarse_list,
):
    groups = PLANES * PLANE
    in_plane = [[z * PLANE + m for m in range(PLANE)] for z in range(PLANES)]
    along_z = [[z * PLANE + m for z in range(PLANES)] for m in range(PLANE)]
    sub = lax.axis_index("sub").reshape(1)
    first_leaf = (lax.axis_index("leaf") * LEAVES).reshape(1)
    four_transfers = transfer.reshape(PARENTS, BRANCH * RANK, RANK)
    four_bases = leaf_cluster_basis.reshape(PARENTS, BRANCH * RANK, ROWS)

    def over_sub(pieces):
        return [pieces[0]] + [
            lax.ppermute(pieces[k], "sub", [(i, (i + k) % SUBS) for i in range(SUBS)])
            for k in range(1, SUBS)
        ]

    wanted, far_index, coarse_index, near_index = call(
        index_kernel,
        "index_tables",
        [
            ((PLANE, LANES), jnp.int32),
            (distant_interaction_list.shape, jnp.int32),
            (coarse_list.shape, jnp.int32),
            (near_list.shape, jnp.int32),
        ],
        of_kind("smem", first_leaf)
        + of_kind("hbm", distant_interaction_list, coarse_list, near_list),
    )
    wanted, sub = lax.optimization_barrier((wanted, sub))
    asked = lax.all_to_all(wanted, "leaf", 0, 0, axis_index_groups=in_plane, tiled=True)

    x_shape = (LEAVES, PROBES, UNKNOWNS)
    edge = (REACH, PROBES, UNKNOWNS)
    tile = (16, LANES)
    message = (PLANES, TILES) + tile
    rows_scratch = [pltpu.VMEM((GOT_ROWS + 1, OWN, LANES), F32)]

    wide_scratch = [pltpu.VMEM((LEAVES + 2 * REACH + 1, PROBES, UNKNOWNS), BF16)]

    def near_args(x, low, high):
        from_below = lax.ppermute(high, "leaf", [(i, i + 1) for i in range(groups - 1)])
        from_above = lax.ppermute(low, "leaf", [(i + 1, i) for i in range(groups - 1)])
        tables = of_kind("smem", near_index)
        return tables + of_kind("vmem", x, from_below, from_above) + of_kind("cut", near_blocks)

    def along(tiles):
        return lax.all_to_all(tiles, "leaf", 0, 0, axis_index_groups=along_z, tiled=True)

    def within(column):
        (chosen,) = call(
            choose_kernel,
            "choose_rows",
            [((PLANE, OUT_TILES) + tile, BF16)],
            of_kind("smem", asked) + of_kind("vmem", column),
            [pltpu.VMEM((PLANES * LEAVES, OWN, LANES), F32)],
        )
        got = lax.all_to_all(chosen, "leaf", 0, 0, axis_index_groups=in_plane, tiled=True)
        return got.reshape((PLANE * OUT_TILES,) + tile)

    packed = call(
        partial_kernel,
        "partial_sums",
        [((PACKED + TILES * 16, LANES), BF16)] * SUBS,
        of_kind("smem", sub) + of_kind("hbm", probes, four_bases, four_transfers),
        [pltpu.VMEM((TILES, PROBES, 4 * RANK), F32)],
    )
    pieces, asked = lax.optimization_barrier((over_sub(packed), asked))
    x0, low, high, tiles = call(
        first_kernel,
        "first_coefficients",
        [(x_shape, BF16), (edge, BF16), (edge, BF16), (message, BF16)],
        of_kind("smem", sub) + of_kind("vmem", *pieces),
        [pltpu.VMEM((SUBS, PACKED, LANES), BF16)],
    )
    column = along(tiles)
    sent = call(
        near_sent_kernel,
        "near_field_sent",
        [((SENT, LANES), BF16)] * SUBS,
        of_kind("smem", sub) + near_args(x0, low, high) + of_kind("hbm", leaf_cluster_basis),
        wide_scratch + [pltpu.VMEM((PROBES, 4 * ROWS), F32)],
        chunks=PARENTS,
    )
    column, sent, later = lax.optimization_barrier((column, sent, sub))
    got = within(column)
    (weights,) = call(
        weights_kernel,
        "join_couplings",
        [((PARENTS + 1, 4 * RANK, FAR * RANK), BF16)],
        of_kind("smem", later) + of_kind("hbm", couplings, coarse_couplings),
    )
    near1, basis = call(
        join_kernel,
        "join_near_basis",
        [((PARENTS, 4 * OWN, UNKNOWNS), BF16), ((PARENTS, 4 * RANK, UNKNOWNS), BF16)],
        of_kind("smem", sub) + of_kind("any", *over_sub(sent)),
        [pltpu.VMEM((SUBS, SENT, LANES), BF16)],
    )
    x1_own, tiles = call(
        middle_kernel,
        "middle",
        [((PARENTS, 4 * OWN, UNKNOWNS), BF16), (message, BF16)],
        of_kind("smem", far_index, coarse_index)
        + of_kind("vmem", got, weights)
        + of_kind("hbm", four_transfers)
        + of_kind("vmem", basis, near1),
        rows_scratch,
    )
    column = along(tiles)
    x1_parts = over_sub([x1_own] * SUBS)
    column, x1_parts = lax.optimization_barrier((column, x1_parts))
    got = within(column)
    x1, low, high, first = call(
        whole_kernel,
        "join_x1",
        [(x_shape, BF16), (edge, BF16), (edge, BF16), (probes.shape, BF16)],
        of_kind("smem", sub) + of_kind("any", *x1_parts),
        [pltpu.VMEM((SUBS, PARENTS, 4 * OWN, UNKNOWNS), BF16)],
    )
    (near2,) = call(
        near_kernel,
        "near_field",
        [((LEAVES, PROBES, ROWS), F32)],
        near_args(x1, low, high),
        wide_scratch,
        chunks=PARENTS,
    )
    got, near2 = lax.optimization_barrier((got, near2))
    (field,) = call(
        last_field_kernel,
        "last_field",
        [((PARENTS,) + tile, BF16)],
        of_kind("smem", far_index, coarse_index)
        + of_kind("vmem", got, weights)
        + of_kind("hbm", four_transfers),
        rows_scratch,
    )
    (second_apply,) = call(
        output_kernel,
        "output",
        [(probes.shape, BF16)],
        of_kind("smem", sub)
        + of_kind("vmem", *over_sub([field] * SUBS))
        + of_kind("any", near2)
        + of_kind("hbm", four_bases),
        [pltpu.VMEM((SUBS, PARENTS) + tile, BF16)],
    )
    return (first, second_apply)


def solution(mesh):
    return jax.shard_map(
        local,
        mesh=mesh,
        in_specs=(
            P(None, "leaf", "sub"),
            P("leaf", None, "sub", None),
            P("leaf", None, "sub"),
            P("leaf", None, None),
            P("leaf", None, None, None),
            P("leaf", None, None, None),
            P("leaf", None),
            P("leaf", None),
            P("leaf", None),
        ),
        out_specs=(P(None, "leaf", "sub"), P(None, "leaf", "sub")),
        check_vma=False,
    )
```

```python
import jax
import jax.numpy as jnp
from jax import lax
from jax.experimental import pallas as pl
from jax.experimental.pallas import tpu as pltpu
from jax.sharding import PartitionSpec as P

RANK = 64
BRANCH = 4
REACH = 4
CAP = 2
LEAVES = 16
PARENTS = 4
PROBES = 32
ROWS = 64
SUBS = 4
OWN = PROBES // SUBS
UNKNOWNS = SUBS * ROWS
NEAR = 9
FAR = 16
PLANES = 8
PLANE = 8
LANES = 128
TILES = PARENTS + 1
LEAF_OUT = PLANES * CAP // 4
OUT_TILES = LEAF_OUT + PLANES
GOT_ROWS = 4 * PLANE * OUT_TILES
PACKED = LEAVES // 2 * PROBES
SENT = 16 * PARENTS + LEAVES // 2 * RANK
BF16, F32 = jnp.bfloat16, jnp.float32

NT = (((1,), (1,)), ((), ()))
VMEM_LIMIT = 16 * 1024 * 1024


def dot(x, y):
    return jnp.dot(x, y, preferred_element_type=F32)


def dot_nt(x, y):
    return lax.dot_general(x, y, NT, preferred_element_type=F32)


class Arriving:
    def __init__(self, source, target, sems, parts):
        size = target.shape[0] // parts
        self.target, self.size, self.pending = target, size, {}
        for c in range(parts):
            part = pl.ds(c * size, size)
            copy = pltpu.make_async_copy(source.at[part], target.at[part], sems.at[c])
            copy.start()
            self.pending[c] = copy

    def finish(self, part=None):
        for c in list(self.pending) if part is None else [part]:
            if c in self.pending:
                self.pending.pop(c).wait()

    def __getitem__(self, index):
        first = index[0] if isinstance(index, tuple) else index
        self.finish(first // self.size if isinstance(first, int) else None)
        return self.target[index]


def call(kernel, name, outs, args, scratch=()):
    spaces = {"smem": pltpu.SMEM, "vmem": pltpu.VMEM, "hbm": pltpu.HBM, "cut": pltpu.HBM, "any": pl.ANY}
    parts = {"hbm": 1, "any": 1, "cut": 4}
    moved = [j for j, (kind, _) in enumerate(args) if kind in parts]
    away = [j for j, out in enumerate(outs) if len(out) == 3]
    scratch = list(scratch)
    buffers = [pltpu.VMEM(args[j][1].shape, args[j][1].dtype) for j in moved]
    buffers += [pltpu.VMEM(outs[j][0], outs[j][1]) for j in away]

    def body(*refs):
        refs = list(refs)
        sems = refs.pop()
        front = len(args) + len(outs) + len(scratch)
        used, arriving = 0, []
        for n, j in enumerate(moved):
            count = parts[args[j][0]]
            refs[j] = Arriving(refs[j], refs[front + n], sems.at[pl.ds(used, count)], count)
            arriving.append(refs[j])
            used += count
        leaving = []
        for n, j in enumerate(away):
            target, source = refs[len(args) + j], refs[front + len(moved) + n]
            leaving.append(pltpu.make_async_copy(source, target, sems.at[used + n]))
            refs[len(args) + j] = source
        kernel(*refs[:front])
        for copy in leaving:
            copy.start()
        for buffer in arriving:
            buffer.finish()
        for copy in leaving:
            copy.wait()

    count = sum(parts[args[j][0]] for j in moved) + len(away)
    return pl.pallas_call(
        body,
        name=name,
        out_shape=[jax.ShapeDtypeStruct(out[0], out[1]) for out in outs],
        in_specs=[pl.BlockSpec(memory_space=spaces[kind]) for kind, _ in args],
        out_specs=[
            pl.BlockSpec(memory_space=pltpu.HBM if j in away else pltpu.VMEM) for j in range(len(outs))
        ],
        scratch_shapes=scratch + buffers + [pltpu.SemaphoreType.DMA((max(count, 1),))],
        compiler_params=pltpu.CompilerParams(vmem_limit_bytes=VMEM_LIMIT),
    )(*[
        pltpu.with_memory_space_constraint(array, pltpu.HBM) if kind in ("hbm", "cut") else array
        for kind, array in args
    ])


def of_kind(kind, *arrays):
    return [(kind, array) for array in arrays]


def lane_block(rows, lanes):
    return lax.broadcasted_iota(jnp.int32, (rows, lanes), 1) // RANK


def diagonal(x, rows):
    block = lane_block(rows, 4 * RANK)
    out = x[:rows]
    for c in range(1, 4):
        out = jnp.where(block == c, x[c * rows : (c + 1) * rows], out)
    return out


def spread_diagonal(x):
    block = lane_block(x.shape[0], 4 * RANK)
    return jnp.concatenate([jnp.where(block == c, x, jnp.zeros_like(x)) for c in range(4)], axis=0)


def to_tile(x):
    return jnp.concatenate([x[:, :LANES], x[:, LANES:]], axis=0).astype(BF16)


def tile_row(tile, c):
    h, g = c // 2, c % 2
    return tile[h * OWN : (h + 1) * OWN, g * RANK : (g + 1) * RANK]


def index_kernel(_, far_ref, coarse_ref, wanted_ref, far_out_ref, coarse_out_ref):
    groups = PLANES * PLANE
    group = lax.broadcasted_iota(jnp.int32, (groups, FAR), 0)
    named = far_ref[...]
    owner = jnp.where(named >= 0, named >> 4, -1)
    place = (named & (LEAVES - 1)).astype(F32)
    hits = [owner[i : i + 1] == group for i in range(LEAVES)]
    least = jnp.full((groups, FAR), LEAVES - 1.0, F32)
    greatest = jnp.zeros((groups, FAR), F32)
    for i in range(LEAVES):
        least = jnp.minimum(least, jnp.where(hits[i], place[i : i + 1], LEAVES - 1.0))
        greatest = jnp.maximum(greatest, jnp.where(hits[i], place[i : i + 1], 0.0))
    least = jnp.min(least, axis=1, keepdims=True)
    greatest = jnp.max(greatest, axis=1, keepdims=True)
    lane = lax.broadcasted_iota(jnp.int32, (PLANE, LANES), 1)
    wanted = jnp.zeros((PLANE, LANES), F32)
    for z in range(PLANES):
        wanted = jnp.where(lane == CAP * z, least[z * PLANE : (z + 1) * PLANE], wanted)
        wanted = jnp.where(lane == CAP * z + 1, greatest[z * PLANE : (z + 1) * PLANE], wanted)
    wanted_ref[...] = wanted.astype(jnp.int32)
    of_entry = [
        jnp.sum(jnp.where(hits[i], least, 0.0), axis=0, keepdims=True) for i in range(LEAVES)
    ]
    second = jnp.where(place == jnp.concatenate(of_entry, axis=0), 0, 1)
    row = (owner & (PLANE - 1)) * (4 * OUT_TILES) + (owner >> 3) * CAP + second
    far_out_ref[...] = jnp.where(named >= 0, row, GOT_ROWS)
    coarse = coarse_ref[...]
    owner = coarse >> 2
    row = (owner & (PLANE - 1)) * (4 * OUT_TILES) + 4 * LEAF_OUT + (owner >> 3) * PARENTS
    coarse_out_ref[...] = jnp.where(coarse >= 0, row + (coarse & (PARENTS - 1)), GOT_ROWS)


def partial_kernel(
    sub_ref, x_ref, basis_ref, transfer_ref, out0_ref, out1_ref, out2_ref, out3_ref, sums_ref
):
    out_refs = [out0_ref, out1_ref, out2_ref, out3_ref]
    x = jnp.transpose(x_ref[...].astype(F32), (1, 0, 2)).astype(BF16)
    for j in range(LEAVES // 2):
        pair = jnp.concatenate([x[2 * j], x[2 * j + 1]], axis=1)
        for out_ref in out_refs:
            out_ref[pl.ds(j * PROBES, PROBES), :] = pair
    parents = []
    sums = []
    for q in range(PARENTS):
        four = x[4 * q : 4 * q + 4].reshape(4 * PROBES, ROWS)
        leaf = diagonal(dot_nt(four, basis_ref[q]), PROBES)
        sums.append(leaf)
        parents.append(dot(leaf.astype(BF16), transfer_ref[q]))
    sums.append(jnp.concatenate(parents, axis=1))
    for t in range(TILES):
        sums_ref[t] = sums[t]
    for k, out_ref in enumerate(out_refs):
        place = probes_of((sub_ref[0] + k) % SUBS)
        for t in range(TILES):
            out_ref[pl.ds(PACKED + 16 * t, 16), :] = to_tile(sums_ref[t, place, :])


def probes_of(sub):
    return pl.ds(pl.multiple_of(sub * OWN, OWN), OWN)


def in_order(sub_ref, piece_refs, slots_ref, rows):
    for k, piece_ref in enumerate(piece_refs):
        slots_ref[(sub_ref[0] + SUBS - k) % SUBS] = piece_ref[pl.ds(0, rows)]


def first_kernel(
    sub_ref, got0_ref, got1_ref, got2_ref, got3_ref, x_ref, low_ref, high_ref, out_ref, slots_ref
):
    got_refs = [got0_ref, got1_ref, got2_ref, got3_ref]
    for t in range(TILES):
        total = got0_ref[pl.ds(PACKED + 16 * t, 16), :].astype(F32)
        for got_ref in got_refs[1:]:
            total = total + got_ref[pl.ds(PACKED + 16 * t, 16), :].astype(F32)
        tile = total.astype(BF16)
        for z in range(PLANES):
            out_ref[z, t] = tile
    in_order(sub_ref, got_refs, slots_ref, PACKED)
    for i in range(LEAVES):
        half = slice((i % 2) * ROWS, (i % 2 + 1) * ROWS)
        rows = pl.ds((i // 2) * PROBES, PROBES)
        x = jnp.concatenate([slots_ref[s, rows, half] for s in range(SUBS)], axis=1)
        x_ref[i] = x
        if i < REACH:
            low_ref[i] = x
        if i >= LEAVES - REACH:
            high_ref[i - (LEAVES - REACH)] = x


def join_kernel(sub_ref, got0_ref, got1_ref, got2_ref, got3_ref, near_ref, basis_ref, slots_ref):
    in_order(sub_ref, [got0_ref, got1_ref, got2_ref, got3_ref], slots_ref, SENT)
    for q in range(PARENTS):
        tiles = [slots_ref[s, pl.ds(16 * q, 16), :].astype(F32) for s in range(SUBS)]
        near = [jnp.concatenate([tile_row(t, c) for t in tiles], axis=1) for c in range(4)]
        near_ref[q] = jnp.concatenate(near, axis=0).astype(BF16)
    for i in range(LEAVES):
        half = slice((i % 2) * ROWS, (i % 2 + 1) * ROWS)
        rows = pl.ds(16 * PARENTS + (i // 2) * RANK, RANK)
        whole = jnp.concatenate([slots_ref[s, rows, half] for s in range(SUBS)], axis=1)
        basis_ref[i // 4, pl.ds(i % 4 * RANK, RANK), :] = whole


def weights_kernel(_, couplings_ref, coarse_ref, out_ref):
    for q in range(PARENTS + 1):
        for c in range(4):
            for k in range(0, FAR, 2):
                if q < PARENTS:
                    pair = [couplings_ref[4 * q + c, k], couplings_ref[4 * q + c, k + 1]]
                else:
                    pair = [coarse_ref[c, k], coarse_ref[c, k + 1]]
                both = jnp.concatenate(pair, axis=1)
                out_ref[q, pl.ds(c * RANK, RANK), pl.ds(k * RANK, LANES)] = both


def both_halves(row_pair):
    turned = pltpu.roll(row_pair, RANK, 1)
    left = lax.broadcasted_iota(jnp.int32, row_pair.shape, 1) < RANK
    return jnp.where(left, row_pair, turned), jnp.where(left, turned, row_pair)


def unpack_tile(tile, rows_ref, first):
    wide = tile.astype(F32)
    for h in range(2):
        one, two = both_halves(wide[h * OWN : (h + 1) * OWN])
        rows_ref[first + 2 * h] = one
        rows_ref[first + 2 * h + 1] = two


def choose_kernel(asked_ref, got_ref, out_ref, rows_ref):
    for z in range(PLANES):
        for t in range(LEAVES // 4):
            unpack_tile(got_ref[z, t], rows_ref, z * LEAVES + 4 * t)
    left = lax.broadcasted_iota(jnp.int32, (OWN, LANES), 1) < RANK
    for m in range(PLANE):
        for t in range(LEAF_OUT):
            rows = []
            for n in range(4 * t, 4 * t + 4):
                rows.append(rows_ref[n // CAP * LEAVES + asked_ref[m, n]])
            top = jnp.where(left, rows[0], rows[1])
            bottom = jnp.where(left, rows[2], rows[3])
            out_ref[m, t] = jnp.concatenate([top, bottom], axis=0).astype(BF16)
        for z in range(PLANES):
            out_ref[m, LEAF_OUT + z] = got_ref[z, TILES - 1]


def far_field(far_ref, coarse_ref, got_ref, weights_ref, transfer_ref, rows_ref):
    for n in range(PLANE * OUT_TILES):
        unpack_tile(got_ref[n], rows_ref, 4 * n)
    rows_ref[GOT_ROWS] = jnp.zeros((OWN, LANES), F32)
    left = lax.broadcasted_iota(jnp.int32, (OWN, LANES), 1) < RANK

    def apply(index_ref, q, weights):
        picked = []
        for c in range(4):
            pairs = []
            for k in range(0, FAR, 2):
                one = rows_ref[index_ref[4 * q + c, k]]
                two = rows_ref[index_ref[4 * q + c, k + 1]]
                pairs.append(jnp.where(left, one, two))
            picked.append(jnp.concatenate(pairs, axis=1))
        picked = jnp.concatenate(picked, axis=0).astype(BF16)
        return diagonal(dot_nt(picked, weights), OWN)

    coarse = apply(coarse_ref, 0, weights_ref[PARENTS]).astype(BF16)
    fields = []
    for q in range(PARENTS):
        down = dot_nt(coarse[:, q * RANK : (q + 1) * RANK], transfer_ref[q])
        fields.append(apply(far_ref, q, weights_ref[q]) + down)
    return fields


def middle_kernel(
    far_ref,
    coarse_ref,
    got_ref,
    weights_ref,
    transfer_ref,
    basis_ref,
    near_ref,
    x_ref,
    out_ref,
    rows_ref,
):
    fields = far_field(far_ref, coarse_ref, got_ref, weights_ref, transfer_ref, rows_ref)
    tiles = []
    parents = []
    for q in range(PARENTS):
        far = dot(spread_diagonal(fields[q]).astype(BF16), basis_ref[q])
        x = (near_ref[q].astype(F32) + far).astype(BF16)
        x_ref[q] = x
        leaf = diagonal(dot_nt(x, basis_ref[q]), OWN)
        tiles.append(to_tile(leaf))
        parents.append(dot(leaf.astype(BF16), transfer_ref[q]))
    tiles.append(to_tile(jnp.concatenate(parents, axis=1)))
    for t in range(TILES):
        for z in range(PLANES):
            out_ref[z, t] = tiles[t]


def last_field_kernel(
    far_ref, coarse_ref, got_ref, weights_ref, transfer_ref, out_ref, rows_ref
):
    fields = far_field(far_ref, coarse_ref, got_ref, weights_ref, transfer_ref, rows_ref)
    for q in range(PARENTS):
        out_ref[q] = to_tile(fields[q])


def whole_kernel(
    sub_ref,
    got0_ref,
    got1_ref,
    got2_ref,
    got3_ref,
    x_ref,
    low_ref,
    high_ref,
    first_ref,
    got_ref,
):
    in_order(sub_ref, [got0_ref, got1_ref, got2_ref, got3_ref], got_ref, PARENTS)
    sub = sub_ref[0]
    outs = []
    for q in range(PARENTS):
        parts = [got_ref[s, q].astype(F32) for s in range(SUBS)]
        for c in range(4):
            i = 4 * q + c
            rows = slice(c * OWN, (c + 1) * OWN)
            wide = jnp.concatenate([part[rows] for part in parts], axis=0)
            x = wide.astype(BF16)
            x_ref[i] = x
            if i < REACH:
                low_ref[i] = x
            if i >= LEAVES - REACH:
                high_ref[i - (LEAVES - REACH)] = x
            mine = wide[:, :ROWS]
            for s in range(1, SUBS):
                mine = jnp.where(sub == s, wide[:, s * ROWS : (s + 1) * ROWS], mine)
            outs.append(mine)
    first_ref[...] = jnp.transpose(jnp.stack(outs), (1, 0, 2)).astype(BF16)


def output_kernel(
    sub_ref, field0_ref, field1_ref, field2_ref, field3_ref, near_ref, basis_ref, out_ref, field_ref
):
    in_order(sub_ref, [field0_ref, field1_ref, field2_ref, field3_ref], field_ref, PARENTS)
    outs = []
    for q in range(PARENTS):
        tiles = [field_ref[s, q].astype(F32) for s in range(SUBS)]
        field = jnp.concatenate(
            [jnp.concatenate([t[:OWN], t[OWN:]], axis=1) for t in tiles], axis=0
        )
        far = dot(spread_diagonal(field).astype(BF16), basis_ref[q])
        for c in range(4):
            outs.append(near_ref[4 * q + c] + far[c * PROBES : (c + 1) * PROBES])
    out_ref[...] = jnp.transpose(jnp.stack(outs), (1, 0, 2)).astype(BF16)


def near_parts(first_ref, list_ref, x_ref, low_ref, high_ref, blocks_ref, wide_ref):
    wide_ref[pl.ds(0, REACH)] = low_ref[...]
    wide_ref[pl.ds(REACH, LEAVES)] = x_ref[...]
    wide_ref[pl.ds(REACH + LEAVES, REACH)] = high_ref[...]
    wide_ref[2 * REACH + LEAVES] = jnp.zeros((PROBES, UNKNOWNS), BF16)

    def of_slot(i, k):
        leaf = list_ref[i, k]
        place = jnp.where(leaf >= 0, leaf - first_ref[0] + REACH, LEAVES + 2 * REACH)
        return wide_ref[place]

    for q in range(PARENTS):
        four = []
        for i in range(4 * q, 4 * q + 4):
            x = jnp.concatenate([of_slot(i, k) for k in range(NEAR)], axis=1)
            blocks = jnp.concatenate([blocks_ref[i, k] for k in range(NEAR)], axis=1)
            four.append(dot_nt(x, blocks))
        yield four


def near_sent_kernel(
    sub_ref,
    first_ref,
    list_ref,
    x_ref,
    low_ref,
    high_ref,
    blocks_ref,
    basis_ref,
    out0_ref,
    out1_ref,
    out2_ref,
    out3_ref,
    wide_ref,
    four_ref,
):
    out_refs = [out0_ref, out1_ref, out2_ref, out3_ref]
    parts = near_parts(first_ref, list_ref, x_ref, low_ref, high_ref, blocks_ref, wide_ref)
    for q, four in enumerate(parts):
        four_ref[...] = jnp.concatenate(four, axis=1)
        for k, out_ref in enumerate(out_refs):
            tile = to_tile(four_ref[probes_of((sub_ref[0] + k) % SUBS), :])
            out_ref[pl.ds(16 * q, 16), :] = tile
    for j in range(LEAVES // 2):
        pair = jnp.concatenate([basis_ref[2 * j], basis_ref[2 * j + 1]], axis=1)
        for out_ref in out_refs:
            out_ref[pl.ds(16 * PARENTS + j * RANK, RANK), :] = pair


def near_kernel(first_ref, list_ref, x_ref, low_ref, high_ref, blocks_ref, out_ref, wide_ref):
    parts = near_parts(first_ref, list_ref, x_ref, low_ref, high_ref, blocks_ref, wide_ref)
    for q, four in enumerate(parts):
        for c in range(4):
            out_ref[4 * q + c] = four[c]


def local(
    probes,
    near_blocks,
    leaf_cluster_basis,
    transfer,
    couplings,
    coarse_couplings,
    near_list,
    distant_interaction_list,
    coarse_list,
):
    groups = PLANES * PLANE
    in_plane = [[z * PLANE + m for m in range(PLANE)] for z in range(PLANES)]
    along_z = [[z * PLANE + m for z in range(PLANES)] for m in range(PLANE)]
    sub = lax.axis_index("sub").reshape(1)
    first_leaf = (lax.axis_index("leaf") * LEAVES).reshape(1)
    four_transfers = transfer.reshape(PARENTS, BRANCH * RANK, RANK)
    four_bases = leaf_cluster_basis.reshape(PARENTS, BRANCH * RANK, ROWS)

    def over_sub(pieces):
        return [pieces[0]] + [
            lax.ppermute(pieces[k], "sub", [(i, (i + k) % SUBS) for i in range(SUBS)])
            for k in range(1, SUBS)
        ]

    x_shape = (LEAVES, PROBES, UNKNOWNS)
    edge = (REACH, PROBES, UNKNOWNS)
    tile = (16, LANES)
    message = (PLANES, TILES) + tile
    rows_scratch = [pltpu.VMEM((GOT_ROWS + 1, OWN, LANES), F32)]

    wide_scratch = [pltpu.VMEM((LEAVES + 2 * REACH + 1, PROBES, UNKNOWNS), BF16)]

    def near_args(x, low, high):
        from_below = lax.ppermute(high, "leaf", [(i, i + 1) for i in range(groups - 1)])
        from_above = lax.ppermute(low, "leaf", [(i + 1, i) for i in range(groups - 1)])
        tables = of_kind("smem", first_leaf, near_list)
        return tables + of_kind("vmem", x, from_below, from_above) + of_kind("cut", near_blocks)

    def along(tiles):
        return lax.all_to_all(tiles, "leaf", 0, 0, axis_index_groups=along_z, tiled=True)

    def within(column, asked):
        (chosen,) = call(
            choose_kernel,
            "choose_rows",
            [((PLANE, OUT_TILES) + tile, BF16, True)],
            of_kind("smem", asked) + of_kind("vmem", column),
            [pltpu.VMEM((PLANES * LEAVES, OWN, LANES), F32)],
        )
        got = lax.all_to_all(chosen, "leaf", 0, 0, axis_index_groups=in_plane, tiled=True)
        return got.reshape((PLANE * OUT_TILES,) + tile)

    packed = call(
        partial_kernel,
        "partial_sums",
        [((PACKED + TILES * 16, LANES), BF16)] * SUBS,
        of_kind("smem", sub) + of_kind("hbm", probes, four_bases, four_transfers),
        [pltpu.VMEM((TILES, PROBES, 4 * RANK), F32)],
    )
    first_leaf, packed = lax.optimization_barrier((first_leaf, packed))
    wanted, far_index, coarse_index = call(
        index_kernel,
        "index_tables",
        [
            ((PLANE, LANES), jnp.int32),
            (distant_interaction_list.shape, jnp.int32),
            (coarse_list.shape, jnp.int32),
        ],
        of_kind("smem", first_leaf) + of_kind("hbm", distant_interaction_list, coarse_list),
    )
    pieces, wanted = lax.optimization_barrier((over_sub(packed), wanted))
    x0, low, high, tiles = call(
        first_kernel,
        "first_coefficients",
        [(x_shape, BF16), (edge, BF16), (edge, BF16), (message, BF16, True)],
        of_kind("smem", sub) + of_kind("vmem", *pieces),
        [pltpu.VMEM((SUBS, PACKED, LANES), BF16)],
    )
    column, wanted = lax.optimization_barrier((along(tiles), wanted))
    asked = lax.all_to_all(wanted, "leaf", 0, 0, axis_index_groups=in_plane, tiled=True)
    sent = call(
        near_sent_kernel,
        "near_field_sent",
        [((SENT, LANES), BF16, True)] + [((SENT, LANES), BF16)] * (SUBS - 1),
        of_kind("smem", sub) + near_args(x0, low, high) + of_kind("hbm", leaf_cluster_basis),
        wide_scratch + [pltpu.VMEM((PROBES, 4 * ROWS), F32)],
    )
    column, sent, later = lax.optimization_barrier((column, sent, sub))
    got = within(column, asked)
    (weights,) = call(
        weights_kernel,
        "join_couplings",
        [((PARENTS + 1, 4 * RANK, FAR * RANK), BF16, True)],
        of_kind("smem", later) + of_kind("cut", couplings, coarse_couplings),
    )
    near1, basis = call(
        join_kernel,
        "join_near_basis",
        [((PARENTS, 4 * OWN, UNKNOWNS), BF16, True), ((PARENTS, 4 * RANK, UNKNOWNS), BF16, True)],
        of_kind("smem", sub) + of_kind("any", *over_sub(sent)),
        [pltpu.VMEM((SUBS, SENT, LANES), BF16)],
    )
    x1_own, tiles = call(
        middle_kernel,
        "middle",
        [((PARENTS, 4 * OWN, UNKNOWNS), BF16, True), (message, BF16, True)],
        of_kind("smem", far_index, coarse_index)
        + of_kind("vmem", got)
        + of_kind("any", weights)
        + of_kind("hbm", four_transfers)
        + of_kind("any", basis, near1),
        rows_scratch,
    )
    got = within(along(tiles), asked)
    x1, low, high, first = call(
        whole_kernel,
        "join_x1",
        [(x_shape, BF16), (edge, BF16), (edge, BF16), (probes.shape, BF16)],
        of_kind("smem", sub) + of_kind("any", *over_sub([x1_own] * SUBS)),
        [pltpu.VMEM((SUBS, PARENTS, 4 * OWN, UNKNOWNS), BF16)],
    )
    (near2,) = call(
        near_kernel,
        "near_field",
        [((LEAVES, PROBES, ROWS), F32)],
        near_args(x1, low, high),
        wide_scratch,
    )
    got, near2 = lax.optimization_barrier((got, near2))
    (field,) = call(
        last_field_kernel,
        "last_field",
        [((PARENTS,) + tile, BF16)],
        of_kind("smem", far_index, coarse_index)
        + of_kind("vmem", got)
        + of_kind("any", weights)
        + of_kind("hbm", four_transfers),
        rows_scratch,
    )
    (second_apply,) = call(
        output_kernel,
        "output",
        [(probes.shape, BF16)],
        of_kind("smem", sub)
        + of_kind("vmem", *over_sub([field] * SUBS))
        + of_kind("vmem", near2, four_bases),
        [pltpu.VMEM((SUBS, PARENTS) + tile, BF16)],
    )
    return (first, second_apply)


def solution(mesh):
    return jax.shard_map(
        local,
        mesh=mesh,
        in_specs=(
            P(None, "leaf", "sub"),
            P("leaf", None, "sub", None),
            P("leaf", None, "sub"),
            P("leaf", None, None),
            P("leaf", None, None, None),
            P("leaf", None, None, None),
            P("leaf", None),
            P("leaf", None),
            P("leaf", None),
        ),
        out_specs=(P(None, "leaf", "sub"), P(None, "leaf", "sub")),
        check_vma=False,
    )
```

```python
import jax
import jax.numpy as jnp
from jax import lax
from jax.experimental import pallas as pl
from jax.experimental.pallas import tpu as pltpu
from jax.sharding import PartitionSpec as P

RANK = 64
BRANCH = 4
REACH = 4
CAP = 2
LEAVES = 16
PARENTS = 4
PROBES = 32
ROWS = 64
SUBS = 4
OWN = PROBES // SUBS
UNKNOWNS = SUBS * ROWS
NEAR = 9
FAR = 16
PLANES = 8
PLANE = 8
LANES = 128
TILES = PARENTS + 1
LEAF_OUT = PLANES * CAP // 4
OUT_TILES = LEAF_OUT + PLANES
GOT_ROWS = 4 * PLANE * OUT_TILES
PACKED = LEAVES // 2 * PROBES
SENT = PACKED + LEAVES // 2 * RANK
BF16, F32 = jnp.bfloat16, jnp.float32

NT = (((1,), (1,)), ((), ()))
VMEM_LIMIT = 16 * 1024 * 1024


def dot(x, y):
    return jnp.dot(x, y, preferred_element_type=F32)


def dot_nt(x, y):
    return lax.dot_general(x, y, NT, preferred_element_type=F32)


class Arriving:
    def __init__(self, source, target, sems, parts):
        size = target.shape[0] // parts
        self.target, self.size, self.pending = target, size, {}
        for c in range(parts):
            part = pl.ds(c * size, size)
            copy = pltpu.make_async_copy(source.at[part], target.at[part], sems.at[c])
            copy.start()
            self.pending[c] = copy

    def finish(self, part=None):
        for c in list(self.pending) if part is None else [part]:
            if c in self.pending:
                self.pending.pop(c).wait()

    def __getitem__(self, index):
        first = index[0] if isinstance(index, tuple) else index
        self.finish(first // self.size if isinstance(first, int) else None)
        return self.target[index]


class Leaving:
    def __init__(self, source, target, sems, parts):
        size = target.shape[0] // parts
        self.source, self.started = source, []
        self.waiting = {}
        for c in range(parts):
            part = pl.ds(c * size, size)
            self.waiting[c] = pltpu.make_async_copy(source.at[part], target.at[part], sems.at[c])

    def __setitem__(self, index, value):
        self.source[index] = value

    def send(self, part=None):
        for c in list(self.waiting) if part is None else [part]:
            copy = self.waiting.pop(c)
            copy.start()
            self.started.append(copy)

    def finish(self):
        self.send()
        for copy in self.started:
            copy.wait()


PARTS = {"hbm": 1, "any": 1, "cut": 4}


def call(kernel, name, outs, args, scratch=()):
    spaces = {"smem": pltpu.SMEM, "table": pltpu.SMEM, "vmem": pltpu.VMEM, "any": pl.ANY}
    moved = [j for j, (kind, _) in enumerate(args) if kind in PARTS]
    away = [j for j, out in enumerate(outs) if len(out) == 3]
    scratch = list(scratch)
    buffers = [pltpu.VMEM(args[j][1].shape, args[j][1].dtype) for j in moved]
    buffers += [pltpu.VMEM(outs[j][0], outs[j][1]) for j in away]

    def body(*refs):
        refs = list(refs)
        sems = refs.pop()
        front = len(args) + len(outs) + len(scratch)
        used = 0
        for n, j in enumerate(moved):
            count = PARTS[args[j][0]]
            refs[j] = Arriving(refs[j], refs[front + n], sems.at[pl.ds(used, count)], count)
            used += count
        for n, j in enumerate(away):
            target, source = refs[len(args) + j], refs[front + len(moved) + n]
            count = outs[j][2]
            refs[len(args) + j] = Leaving(source, target, sems.at[pl.ds(used, count)], count)
            used += count
        kernel(*refs[:front])
        for ref in refs[:front]:
            if isinstance(ref, (Arriving, Leaving)):
                ref.finish()

    count = sum(PARTS[args[j][0]] for j in moved) + sum(outs[j][2] for j in away)
    return pl.pallas_call(
        body,
        name=name,
        out_shape=[
            pltpu.HBM(out[0], out[1]) if len(out) == 3 else jax.ShapeDtypeStruct(*out) for out in outs
        ],
        in_specs=[pl.BlockSpec(memory_space=spaces.get(kind, pltpu.HBM)) for kind, _ in args],
        out_specs=[
            pl.BlockSpec(memory_space=pltpu.HBM if j in away else pltpu.VMEM) for j in range(len(outs))
        ],
        scratch_shapes=scratch + buffers + [pltpu.SemaphoreType.DMA((max(count, 1),))],
        compiler_params=pltpu.CompilerParams(vmem_limit_bytes=VMEM_LIMIT),
    )(*[
        array if kind in ("smem", "vmem", "any") else pltpu.with_memory_space_constraint(array, pltpu.HBM)
        for kind, array in args
    ])


def of_kind(kind, *arrays):
    return [(kind, array) for array in arrays]


def lane_block(rows, lanes):
    return lax.broadcasted_iota(jnp.int32, (rows, lanes), 1) // RANK


def diagonal(x, rows):
    block = lane_block(rows, 4 * RANK)
    out = x[:rows]
    for c in range(1, 4):
        out = jnp.where(block == c, x[c * rows : (c + 1) * rows], out)
    return out


def spread_diagonal(x):
    block = lane_block(x.shape[0], 4 * RANK)
    return jnp.concatenate([jnp.where(block == c, x, jnp.zeros_like(x)) for c in range(4)], axis=0)


def to_tile(x):
    return jnp.concatenate([x[:, :LANES], x[:, LANES:]], axis=0).astype(BF16)


def index_kernel(_, far_ref, coarse_ref, wanted_ref, far_out_ref, coarse_out_ref):
    groups = PLANES * PLANE
    group = lax.broadcasted_iota(jnp.int32, (groups, FAR), 0)
    named = far_ref[...]
    owner = jnp.where(named >= 0, named >> 4, -1)
    place = (named & (LEAVES - 1)).astype(F32)
    hits = [owner[i : i + 1] == group for i in range(LEAVES)]
    least = jnp.full((groups, FAR), LEAVES - 1.0, F32)
    greatest = jnp.zeros((groups, FAR), F32)
    for i in range(LEAVES):
        least = jnp.minimum(least, jnp.where(hits[i], place[i : i + 1], LEAVES - 1.0))
        greatest = jnp.maximum(greatest, jnp.where(hits[i], place[i : i + 1], 0.0))
    least = jnp.min(least, axis=1, keepdims=True)
    greatest = jnp.max(greatest, axis=1, keepdims=True)
    lane = lax.broadcasted_iota(jnp.int32, (PLANE, LANES), 1)
    wanted = jnp.zeros((PLANE, LANES), F32)
    for z in range(PLANES):
        wanted = jnp.where(lane == CAP * z, least[z * PLANE : (z + 1) * PLANE], wanted)
        wanted = jnp.where(lane == CAP * z + 1, greatest[z * PLANE : (z + 1) * PLANE], wanted)
    wanted_ref[...] = wanted.astype(jnp.int32)
    of_entry = [
        jnp.sum(jnp.where(hits[i], least, 0.0), axis=0, keepdims=True) for i in range(LEAVES)
    ]
    second = jnp.where(place == jnp.concatenate(of_entry, axis=0), 0, 1)
    row = (owner & (PLANE - 1)) * (4 * OUT_TILES) + (owner >> 3) * CAP + second
    far_out_ref[...] = jnp.where(named >= 0, row, GOT_ROWS)
    coarse = coarse_ref[...]
    owner = coarse >> 2
    row = (owner & (PLANE - 1)) * (4 * OUT_TILES) + 4 * LEAF_OUT + (owner >> 3) * PARENTS
    coarse_out_ref[...] = jnp.where(coarse >= 0, row + (coarse & (PARENTS - 1)), GOT_ROWS)


def partial_kernel(
    sub_ref, x_ref, basis_ref, transfer_ref, out0_ref, out1_ref, out2_ref, out3_ref, sums_ref
):
    out_refs = [out0_ref, out1_ref, out2_ref, out3_ref]
    x = jnp.transpose(x_ref[...].astype(F32), (1, 0, 2)).astype(BF16)
    for j in range(LEAVES // 2):
        pair = jnp.concatenate([x[2 * j], x[2 * j + 1]], axis=1)
        for out_ref in out_refs:
            out_ref[pl.ds(j * PROBES, PROBES), :] = pair
    parents = []
    sums = []
    for q in range(PARENTS):
        four = x[4 * q : 4 * q + 4].reshape(4 * PROBES, ROWS)
        leaf = diagonal(dot_nt(four, basis_ref[q]), PROBES)
        sums.append(leaf)
        parents.append(dot(leaf.astype(BF16), transfer_ref[q]))
    sums.append(jnp.concatenate(parents, axis=1))
    for t in range(TILES):
        sums_ref[t] = sums[t]
    for k, out_ref in enumerate(out_refs):
        place = probes_of((sub_ref[0] + k) % SUBS)
        for t in range(TILES):
            out_ref[pl.ds(PACKED + 16 * t, 16), :] = to_tile(sums_ref[t, place, :])


def probes_of(sub):
    return pl.ds(pl.multiple_of(sub * OWN, OWN), OWN)


def in_order(sub_ref, piece_refs, slots_ref, rows):
    for k, piece_ref in enumerate(piece_refs):
        slots_ref[(sub_ref[0] + SUBS - k) % SUBS] = piece_ref[pl.ds(0, rows)]


def first_kernel(
    sub_ref, got0_ref, got1_ref, got2_ref, got3_ref, x_ref, low_ref, high_ref, out_ref, slots_ref
):
    got_refs = [got0_ref, got1_ref, got2_ref, got3_ref]
    for t in range(TILES):
        total = got0_ref[pl.ds(PACKED + 16 * t, 16), :].astype(F32)
        for got_ref in got_refs[1:]:
            total = total + got_ref[pl.ds(PACKED + 16 * t, 16), :].astype(F32)
        tile = total.astype(BF16)
        for z in range(PLANES):
            out_ref[z, t] = tile
    out_ref.send()
    in_order(sub_ref, got_refs, slots_ref, PACKED)
    for i in range(LEAVES):
        half = slice((i % 2) * ROWS, (i % 2 + 1) * ROWS)
        rows = pl.ds((i // 2) * PROBES, PROBES)
        x = jnp.concatenate([slots_ref[s, rows, half] for s in range(SUBS)], axis=1)
        x_ref[i] = x
        if i < REACH:
            low_ref[i] = x
        if i >= LEAVES - REACH:
            high_ref[i - (LEAVES - REACH)] = x


def join_kernel(sub_ref, got0_ref, got1_ref, got2_ref, got3_ref, near_ref, basis_ref, slots_ref):
    in_order(sub_ref, [got0_ref, got1_ref, got2_ref, got3_ref], slots_ref, SENT)

    def whole(i, start, size):
        half = slice((i % 2) * ROWS, (i % 2 + 1) * ROWS)
        rows = pl.ds(start + (i // 2) * size, size)
        return jnp.concatenate([slots_ref[s, rows, half] for s in range(SUBS)], axis=1)

    for i in range(LEAVES):
        near_ref[i // 4, pl.ds(i % 4 * PROBES, PROBES), :] = whole(i, 0, PROBES)
        basis_ref[i // 4, pl.ds(i % 4 * RANK, RANK), :] = whole(i, PACKED, RANK)


def weights_kernel(_, couplings_ref, coarse_ref, out_ref):
    for q in range(PARENTS + 1):
        for c in range(4):
            for k in range(0, FAR, 2):
                if q < PARENTS:
                    pair = [couplings_ref[4 * q + c, k], couplings_ref[4 * q + c, k + 1]]
                else:
                    pair = [coarse_ref[c, k], coarse_ref[c, k + 1]]
                both = jnp.concatenate(pair, axis=1)
                out_ref[q, pl.ds(c * RANK, RANK), pl.ds(k * RANK, LANES)] = both


def both_halves(row_pair):
    turned = pltpu.roll(row_pair, RANK, 1)
    left = lax.broadcasted_iota(jnp.int32, row_pair.shape, 1) < RANK
    return jnp.where(left, row_pair, turned), jnp.where(left, turned, row_pair)


def unpack_tile(tile, rows_ref, first):
    wide = tile.astype(F32)
    for h in range(2):
        one, two = both_halves(wide[h * OWN : (h + 1) * OWN])
        rows_ref[first + 2 * h] = one
        rows_ref[first + 2 * h + 1] = two


def choose_kernel(asked_ref, got_ref, out_ref, rows_ref):
    for z in range(PLANES):
        for t in range(LEAVES // 4):
            unpack_tile(got_ref[z, t], rows_ref, z * LEAVES + 4 * t)
    left = lax.broadcasted_iota(jnp.int32, (OWN, LANES), 1) < RANK
    for m in range(PLANE):
        for t in range(LEAF_OUT):
            rows = []
            for n in range(4 * t, 4 * t + 4):
                rows.append(rows_ref[n // CAP * LEAVES + asked_ref[m, n]])
            top = jnp.where(left, rows[0], rows[1])
            bottom = jnp.where(left, rows[2], rows[3])
            out_ref[m, t] = jnp.concatenate([top, bottom], axis=0).astype(BF16)
        for z in range(PLANES):
            out_ref[m, LEAF_OUT + z] = got_ref[z, TILES - 1]
        if m % 4 == 3:
            out_ref.send(m // 4)


def far_field(far_ref, coarse_ref, got_ref, weights_ref, transfer_ref, rows_ref):
    for n in range(PLANE * OUT_TILES):
        unpack_tile(got_ref[n], rows_ref, 4 * n)
    rows_ref[GOT_ROWS] = jnp.zeros((OWN, LANES), F32)
    left = lax.broadcasted_iota(jnp.int32, (OWN, LANES), 1) < RANK

    def apply(index_ref, q, weights):
        picked = []
        for c in range(4):
            pairs = []
            for k in range(0, FAR, 2):
                one = rows_ref[index_ref[4 * q + c, k]]
                two = rows_ref[index_ref[4 * q + c, k + 1]]
                pairs.append(jnp.where(left, one, two))
            picked.append(jnp.concatenate(pairs, axis=1))
        picked = jnp.concatenate(picked, axis=0).astype(BF16)
        return diagonal(dot_nt(picked, weights), OWN)

    coarse = apply(coarse_ref, 0, weights_ref[PARENTS]).astype(BF16)
    fields = []
    for q in range(PARENTS):
        down = dot_nt(coarse[:, q * RANK : (q + 1) * RANK], transfer_ref[q])
        fields.append(apply(far_ref, q, weights_ref[q]) + down)
    return fields


def field_kernel(
    far_ref, coarse_ref, got_ref, weights_ref, transfer_ref, out_ref, rows_ref
):
    fields = far_field(far_ref, coarse_ref, got_ref, weights_ref, transfer_ref, rows_ref)
    for q in range(PARENTS):
        out_ref[q] = to_tile(fields[q])


def field_of(field_ref, q):
    tiles = [field_ref[s, q].astype(F32) for s in range(SUBS)]
    field = [jnp.concatenate([t[:OWN], t[OWN:]], axis=1) for t in tiles]
    return spread_diagonal(jnp.concatenate(field, axis=0)).astype(BF16)


def second_kernel(
    sub_ref,
    field0_ref,
    field1_ref,
    field2_ref,
    field3_ref,
    near_ref,
    basis_ref,
    transfer_ref,
    x_ref,
    low_ref,
    high_ref,
    out_ref,
    field_ref,
    four_ref,
):
    in_order(sub_ref, [field0_ref, field1_ref, field2_ref, field3_ref], field_ref, PARENTS)
    own = probes_of(sub_ref[0])
    tiles = []
    parents = []
    for q in range(PARENTS):
        far = dot(field_of(field_ref, q), basis_ref[q])
        x = near_ref[q].astype(F32) + far
        mine = []
        for c in range(4):
            i = 4 * q + c
            four_ref[c] = x[c * PROBES : (c + 1) * PROBES]
            mine.append(four_ref[c, own, :])
            leaf = x[c * PROBES : (c + 1) * PROBES].astype(BF16)
            x_ref[i] = leaf
            if i < REACH:
                low_ref[i] = leaf
            if i >= LEAVES - REACH:
                high_ref[i - (LEAVES - REACH)] = leaf
        x_ref.send(q)
        mine = jnp.concatenate(mine, axis=0).astype(BF16)
        leaf = diagonal(dot_nt(mine, basis_ref[q]), OWN)
        tiles.append(to_tile(leaf))
        parents.append(dot(leaf.astype(BF16), transfer_ref[q]))
    tiles.append(to_tile(jnp.concatenate(parents, axis=1)))
    for t in range(TILES):
        for z in range(PLANES):
            out_ref[z, t] = tiles[t]


def output_kernel(
    sub_ref, field0_ref, field1_ref, field2_ref, field3_ref, near_ref, basis_ref, out_ref, field_ref
):
    in_order(sub_ref, [field0_ref, field1_ref, field2_ref, field3_ref], field_ref, PARENTS)
    outs = []
    for q in range(PARENTS):
        far = dot(field_of(field_ref, q), basis_ref[q])
        for c in range(4):
            outs.append(near_ref[4 * q + c] + far[c * PROBES : (c + 1) * PROBES])
    out_ref[...] = jnp.transpose(jnp.stack(outs), (1, 0, 2)).astype(BF16)


def near_parts(first_ref, list_ref, x_ref, low_ref, high_ref, blocks_ref, wide_ref):
    wide_ref[pl.ds(0, REACH)] = low_ref[...]
    wide_ref[pl.ds(REACH, LEAVES)] = x_ref[...]
    wide_ref[pl.ds(REACH + LEAVES, REACH)] = high_ref[...]
    wide_ref[2 * REACH + LEAVES] = jnp.zeros((PROBES, UNKNOWNS), BF16)

    def of_slot(i, k):
        leaf = list_ref[i, k]
        place = jnp.where(leaf >= 0, leaf - first_ref[0] + REACH, LEAVES + 2 * REACH)
        return wide_ref[place]

    for q in range(PARENTS):
        four = []
        for i in range(4 * q, 4 * q + 4):
            x = jnp.concatenate([of_slot(i, k) for k in range(NEAR)], axis=1)
            blocks = jnp.concatenate([blocks_ref[i, k] for k in range(NEAR)], axis=1)
            four.append(dot_nt(x, blocks))
        yield four


def near_sent_kernel(
    first_ref, list_ref, x_ref, low_ref, high_ref, blocks_ref, basis_ref, out_ref, wide_ref
):
    parts = near_parts(first_ref, list_ref, x_ref, low_ref, high_ref, blocks_ref, wide_ref)
    for q, four in enumerate(parts):
        for j in range(2):
            pair = jnp.concatenate(four[2 * j : 2 * j + 2], axis=1).astype(BF16)
            out_ref[pl.ds((2 * q + j) * PROBES, PROBES), :] = pair
    for j in range(LEAVES // 2):
        pair = jnp.concatenate([basis_ref[2 * j], basis_ref[2 * j + 1]], axis=1)
        out_ref[pl.ds(PACKED + j * RANK, RANK), :] = pair


def near_kernel(
    sub_ref, first_ref, list_ref, x_ref, low_ref, high_ref, blocks_ref, out_ref, mine_ref, wide_ref
):
    parts = near_parts(first_ref, list_ref, x_ref, low_ref, high_ref, blocks_ref, wide_ref)
    for q, four in enumerate(parts):
        for c in range(4):
            out_ref[4 * q + c] = four[c]
    outs = []
    for i in range(LEAVES):
        x = x_ref[i].astype(F32)
        mine = x[:, :ROWS]
        for s in range(1, SUBS):
            mine = jnp.where(sub_ref[0] == s, x[:, s * ROWS : (s + 1) * ROWS], mine)
        outs.append(mine)
    mine_ref[...] = jnp.transpose(jnp.stack(outs), (1, 0, 2)).astype(BF16)


def local(
    probes,
    near_blocks,
    leaf_cluster_basis,
    transfer,
    couplings,
    coarse_couplings,
    near_list,
    distant_interaction_list,
    coarse_list,
):
    groups = PLANES * PLANE
    in_plane = [[z * PLANE + m for m in range(PLANE)] for z in range(PLANES)]
    along_z = [[z * PLANE + m for z in range(PLANES)] for m in range(PLANE)]
    sub = lax.axis_index("sub").reshape(1)
    first_leaf = (lax.axis_index("leaf") * LEAVES).reshape(1)
    four_transfers = transfer.reshape(PARENTS, BRANCH * RANK, RANK)
    four_bases = leaf_cluster_basis.reshape(PARENTS, BRANCH * RANK, ROWS)

    def over_sub(pieces):
        return [pieces[0]] + [
            lax.ppermute(pieces[k], "sub", [(i, (i + k) % SUBS) for i in range(SUBS)])
            for k in range(1, SUBS)
        ]

    x_shape = (LEAVES, PROBES, UNKNOWNS)
    edge = (REACH, PROBES, UNKNOWNS)
    tile = (16, LANES)
    message = (PLANES, TILES) + tile
    rows_scratch = [pltpu.VMEM((GOT_ROWS + 1, OWN, LANES), F32)]

    wide_scratch = [pltpu.VMEM((LEAVES + 2 * REACH + 1, PROBES, UNKNOWNS), BF16)]

    def halos(low, high):
        from_below = lax.ppermute(high, "leaf", [(i, i + 1) for i in range(groups - 1)])
        from_above = lax.ppermute(low, "leaf", [(i + 1, i) for i in range(groups - 1)])
        return from_below, from_above

    def near_args(x, from_below, from_above):
        tables = of_kind("smem", first_leaf) + of_kind("table", near_list)
        edges = of_kind("vmem", from_below, from_above)
        return tables + of_kind("hbm", x) + edges + of_kind("cut", near_blocks)

    def along(tiles):
        return lax.all_to_all(tiles, "leaf", 0, 0, axis_index_groups=along_z, tiled=True)

    def within(column, asked):
        (chosen,) = call(
            choose_kernel,
            "choose_rows",
            [((PLANE, OUT_TILES) + tile, BF16, 2)],
            of_kind("smem", asked) + of_kind("vmem", column),
            [pltpu.VMEM((PLANES * LEAVES, OWN, LANES), F32)],
        )
        got = lax.all_to_all(chosen, "leaf", 0, 0, axis_index_groups=in_plane, tiled=True)
        return got.reshape((PLANE * OUT_TILES,) + tile)

    packed = call(
        partial_kernel,
        "partial_sums",
        [((PACKED + TILES * 16, LANES), BF16)] * SUBS,
        of_kind("smem", sub) + of_kind("hbm", probes, four_bases, four_transfers),
        [pltpu.VMEM((TILES, PROBES, 4 * RANK), F32)],
    )
    first_leaf, packed = lax.optimization_barrier((first_leaf, packed))
    wanted, far_index, coarse_index = call(
        index_kernel,
        "index_tables",
        [
            ((PLANE, LANES), jnp.int32),
            (distant_interaction_list.shape, jnp.int32, 1),
            (coarse_list.shape, jnp.int32, 1),
        ],
        of_kind("smem", first_leaf) + of_kind("hbm", distant_interaction_list, coarse_list),
    )
    pieces, wanted = lax.optimization_barrier((over_sub(packed), wanted))
    x0, low, high, tiles = call(
        first_kernel,
        "first_coefficients",
        [(x_shape, BF16, 1), (edge, BF16), (edge, BF16), (message, BF16, 1)],
        of_kind("smem", sub) + of_kind("vmem", *pieces),
        [pltpu.VMEM((SUBS, PACKED, LANES), BF16)],
    )
    column, wanted = lax.optimization_barrier((along(tiles), wanted))
    asked = lax.all_to_all(wanted, "leaf", 0, 0, axis_index_groups=in_plane, tiled=True)
    (sent,) = call(
        near_sent_kernel,
        "near_field_sent",
        [((SENT, LANES), BF16, 1)],
        near_args(x0, *halos(low, high)) + of_kind("hbm", leaf_cluster_basis),
        wide_scratch,
    )
    column, sent, later = lax.optimization_barrier((column, sent, sub))
    got = within(column, asked)
    (weights,) = call(
        weights_kernel,
        "join_couplings",
        [((PARENTS + 1, 4 * RANK, FAR * RANK), BF16)],
        of_kind("smem", later) + of_kind("cut", couplings, coarse_couplings),
    )

    def far(got):
        (field,) = call(
            field_kernel,
            "far_field",
            [((PARENTS,) + tile, BF16)],
            of_kind("table", far_index, coarse_index)
            + of_kind("vmem", got, weights, four_transfers),
            rows_scratch,
        )
        return field

    field_scratch = pltpu.VMEM((SUBS, PARENTS) + tile, BF16)
    field1, pieces = far(got), over_sub([sent] * SUBS)
    near1, basis = call(
        join_kernel,
        "join_near_basis",
        [((PARENTS, 4 * PROBES, UNKNOWNS), BF16), ((PARENTS, 4 * RANK, UNKNOWNS), BF16)],
        of_kind("smem", sub) + of_kind("hbm", pieces[0]) + of_kind("any", *pieces[1:]),
        [pltpu.VMEM((SUBS, SENT, LANES), BF16)],
    )
    x1, low, high, tiles = call(
        second_kernel,
        "second_coefficients",
        [(x_shape, BF16, 4), (edge, BF16), (edge, BF16), (message, BF16, 1)],
        of_kind("smem", sub)
        + of_kind("vmem", *over_sub([field1] * SUBS))
        + of_kind("vmem", near1, basis, four_transfers),
        [field_scratch, pltpu.VMEM((4, PROBES, UNKNOWNS), F32)],
    )
    column, edges = lax.optimization_barrier((along(tiles), halos(low, high)))
    got = within(column, asked)
    near2, first = call(
        near_kernel,
        "near_field",
        [((LEAVES, PROBES, ROWS), F32), (probes.shape, BF16)],
        of_kind("smem", sub) + near_args(x1, *edges),
        wide_scratch,
    )
    got, near2 = lax.optimization_barrier((got, near2))
    (second_apply,) = call(
        output_kernel,
        "output",
        [(probes.shape, BF16)],
        of_kind("smem", sub)
        + of_kind("vmem", *over_sub([far(got)] * SUBS))
        + of_kind("vmem", near2, four_bases),
        [field_scratch],
    )
    return (first, second_apply)


def solution(mesh):
    return jax.shard_map(
        local,
        mesh=mesh,
        in_specs=(
            P(None, "leaf", "sub"),
            P("leaf", None, "sub", None),
            P("leaf", None, "sub"),
            P("leaf", None, None),
            P("leaf", None, None, None),
            P("leaf", None, None, None),
            P("leaf", None),
            P("leaf", None),
            P("leaf", None),
        ),
        out_specs=(P(None, "leaf", "sub"), P(None, "leaf", "sub")),
        check_vma=False,
    )
```

```python
import jax
import jax.numpy as jnp
from jax import lax
from jax.experimental import pallas as pl
from jax.experimental.pallas import tpu as pltpu
from jax.sharding import PartitionSpec as P

RANK = 64
BRANCH = 4
REACH = 4
CAP = 2
LEAVES = 16
PARENTS = 4
PROBES = 32
ROWS = 64
SUBS = 4
OWN = PROBES // SUBS
UNKNOWNS = SUBS * ROWS
NEAR = 9
FAR = 16
PLANES = 8
PLANE = 8
LANES = 128
TILES = PARENTS + 1
LEAF_OUT = PLANES * CAP // 4
OUT_TILES = LEAF_OUT + PLANES
GOT_ROWS = 4 * PLANE * OUT_TILES
PACKED = LEAVES // 2 * PROBES
SENT = PACKED + LEAVES // 2 * RANK
BF16, F32 = jnp.bfloat16, jnp.float32

NT = (((1,), (1,)), ((), ()))
VMEM_LIMIT = 16 * 1024 * 1024


def dot(x, y):
    return jnp.dot(x, y, preferred_element_type=F32)


def dot_nt(x, y):
    return lax.dot_general(x, y, NT, preferred_element_type=F32)


class Arriving:
    def __init__(self, source, target, sems, parts):
        size = target.shape[0] // parts
        self.target, self.size, self.pending = target, size, {}
        for c in range(parts):
            part = pl.ds(c * size, size)
            copy = pltpu.make_async_copy(source.at[part], target.at[part], sems.at[c])
            copy.start()
            self.pending[c] = copy

    def finish(self, part=None):
        for c in list(self.pending) if part is None else [part]:
            if c in self.pending:
                self.pending.pop(c).wait()

    def __getitem__(self, index):
        first = index[0] if isinstance(index, tuple) else index
        if isinstance(first, slice) and first.start is not None:
            first = first.start
        self.finish(first // self.size if isinstance(first, int) else None)
        return self.target[index]


class Leaving:
    def __init__(self, source, target, sems, parts):
        size = target.shape[0] // parts
        self.source, self.started = source, []
        self.waiting = {}
        for c in range(parts):
            part = pl.ds(c * size, size)
            self.waiting[c] = pltpu.make_async_copy(source.at[part], target.at[part], sems.at[c])

    def __setitem__(self, index, value):
        self.source[index] = value

    def send(self, part=None):
        for c in list(self.waiting) if part is None else [part]:
            copy = self.waiting.pop(c)
            copy.start()
            self.started.append(copy)

    def finish(self):
        self.send()
        for copy in self.started:
            copy.wait()


PARTS = {"hbm": 1, "any": 1, "cut": 4}


def call(kernel, name, outs, args, scratch=()):
    spaces = {"smem": pltpu.SMEM, "table": pltpu.SMEM, "vmem": pltpu.VMEM, "any": pl.ANY}
    moved = [j for j, (kind, _) in enumerate(args) if kind in PARTS]
    away = [j for j, out in enumerate(outs) if len(out) == 3]
    scratch = list(scratch)
    buffers = [pltpu.VMEM(args[j][1].shape, args[j][1].dtype) for j in moved]
    buffers += [pltpu.VMEM(outs[j][0], outs[j][1]) for j in away]

    def body(*refs):
        refs = list(refs)
        sems = refs.pop()
        front = len(args) + len(outs) + len(scratch)
        used = 0
        for n, j in enumerate(moved):
            count = PARTS[args[j][0]]
            refs[j] = Arriving(refs[j], refs[front + n], sems.at[pl.ds(used, count)], count)
            used += count
        for n, j in enumerate(away):
            target, source = refs[len(args) + j], refs[front + len(moved) + n]
            count = outs[j][2]
            refs[len(args) + j] = Leaving(source, target, sems.at[pl.ds(used, count)], count)
            used += count
        kernel(*refs[:front])
        for ref in refs[:front]:
            if isinstance(ref, (Arriving, Leaving)):
                ref.finish()

    count = sum(PARTS[args[j][0]] for j in moved) + sum(outs[j][2] for j in away)
    return pl.pallas_call(
        body,
        name=name,
        out_shape=[
            pltpu.HBM(out[0], out[1]) if len(out) == 3 else jax.ShapeDtypeStruct(*out) for out in outs
        ],
        in_specs=[pl.BlockSpec(memory_space=spaces.get(kind, pltpu.HBM)) for kind, _ in args],
        out_specs=[
            pl.BlockSpec(memory_space=pltpu.HBM if j in away else pltpu.VMEM) for j in range(len(outs))
        ],
        scratch_shapes=scratch + buffers + [pltpu.SemaphoreType.DMA((max(count, 1),))],
        compiler_params=pltpu.CompilerParams(vmem_limit_bytes=VMEM_LIMIT),
    )(*[
        array if kind in ("smem", "vmem", "any") else pltpu.with_memory_space_constraint(array, pltpu.HBM)
        for kind, array in args
    ])


def of_kind(kind, *arrays):
    return [(kind, array) for array in arrays]


def lane_block(rows, lanes):
    return lax.broadcasted_iota(jnp.int32, (rows, lanes), 1) // RANK


def diagonal(x, rows):
    block = lane_block(rows, 4 * RANK)
    out = x[:rows]
    for c in range(1, 4):
        out = jnp.where(block == c, x[c * rows : (c + 1) * rows], out)
    return out


def spread_diagonal(x):
    block = lane_block(x.shape[0], 4 * RANK)
    return jnp.concatenate([jnp.where(block == c, x, jnp.zeros_like(x)) for c in range(4)], axis=0)


def to_tile(x):
    return jnp.concatenate([x[:, :LANES], x[:, LANES:]], axis=0).astype(BF16)


def index_kernel(_, far_ref, coarse_ref, wanted_ref, far_out_ref, coarse_out_ref):
    groups = PLANES * PLANE
    group = lax.broadcasted_iota(jnp.int32, (groups, FAR), 0)
    named = far_ref[...]
    owner = jnp.where(named >= 0, named >> 4, -1)
    place = (named & (LEAVES - 1)).astype(F32)
    hits = [owner[i : i + 1] == group for i in range(LEAVES)]
    least = jnp.full((groups, FAR), LEAVES - 1.0, F32)
    greatest = jnp.zeros((groups, FAR), F32)
    for i in range(LEAVES):
        least = jnp.minimum(least, jnp.where(hits[i], place[i : i + 1], LEAVES - 1.0))
        greatest = jnp.maximum(greatest, jnp.where(hits[i], place[i : i + 1], 0.0))
    least = jnp.min(least, axis=1, keepdims=True)
    greatest = jnp.max(greatest, axis=1, keepdims=True)
    lane = lax.broadcasted_iota(jnp.int32, (PLANE, LANES), 1)
    wanted = jnp.zeros((PLANE, LANES), F32)
    for z in range(PLANES):
        wanted = jnp.where(lane == CAP * z, least[z * PLANE : (z + 1) * PLANE], wanted)
        wanted = jnp.where(lane == CAP * z + 1, greatest[z * PLANE : (z + 1) * PLANE], wanted)
    wanted_ref[...] = wanted.astype(jnp.int32)
    of_entry = [
        jnp.sum(jnp.where(hits[i], least, 0.0), axis=0, keepdims=True) for i in range(LEAVES)
    ]
    second = jnp.where(place == jnp.concatenate(of_entry, axis=0), 0, 1)
    row = (owner & (PLANE - 1)) * (4 * OUT_TILES) + (owner >> 3) * CAP + second
    far_out_ref[...] = jnp.where(named >= 0, row, GOT_ROWS)
    coarse = coarse_ref[...]
    owner = coarse >> 2
    row = (owner & (PLANE - 1)) * (4 * OUT_TILES) + 4 * LEAF_OUT + (owner >> 3) * PARENTS
    coarse_out_ref[...] = jnp.where(coarse >= 0, row + (coarse & (PARENTS - 1)), GOT_ROWS)


def partial_kernel(
    sub_ref, x_ref, basis_ref, transfer_ref, out0_ref, out1_ref, out2_ref, out3_ref, sums_ref
):
    out_refs = [out0_ref, out1_ref, out2_ref, out3_ref]
    x = jnp.transpose(x_ref[...].astype(F32), (1, 0, 2)).astype(BF16)
    for j in range(LEAVES // 2):
        pair = jnp.concatenate([x[2 * j], x[2 * j + 1]], axis=1)
        for out_ref in out_refs:
            out_ref[pl.ds(j * PROBES, PROBES), :] = pair
    parents = []
    sums = []
    for q in range(PARENTS):
        four = x[4 * q : 4 * q + 4].reshape(4 * PROBES, ROWS)
        leaf = diagonal(dot_nt(four, basis_ref[q]), PROBES)
        sums.append(leaf)
        parents.append(dot(leaf.astype(BF16), transfer_ref[q]))
    sums.append(jnp.concatenate(parents, axis=1))
    for t in range(TILES):
        sums_ref[t] = sums[t]
    for k, out_ref in enumerate(out_refs):
        place = probes_of((sub_ref[0] + k) % SUBS)
        for t in range(TILES):
            out_ref[pl.ds(PACKED + 16 * t, 16), :] = to_tile(sums_ref[t, place, :])


def probes_of(sub):
    return pl.ds(pl.multiple_of(sub * OWN, OWN), OWN)


def in_order(sub_ref, piece_refs, slots_ref, rows):
    for k, piece_ref in enumerate(piece_refs):
        slots_ref[(sub_ref[0] + SUBS - k) % SUBS] = piece_ref[pl.ds(0, rows)]


def first_kernel(
    sub_ref, got0_ref, got1_ref, got2_ref, got3_ref, x_ref, low_ref, high_ref, out_ref, slots_ref
):
    got_refs = [got0_ref, got1_ref, got2_ref, got3_ref]
    for t in range(TILES):
        total = got0_ref[pl.ds(PACKED + 16 * t, 16), :].astype(F32)
        for got_ref in got_refs[1:]:
            total = total + got_ref[pl.ds(PACKED + 16 * t, 16), :].astype(F32)
        tile = total.astype(BF16)
        for z in range(PLANES):
            out_ref[z, t] = tile
    out_ref.send()
    in_order(sub_ref, got_refs, slots_ref, PACKED)
    for i in range(LEAVES):
        half = slice((i % 2) * ROWS, (i % 2 + 1) * ROWS)
        rows = pl.ds((i // 2) * PROBES, PROBES)
        x = jnp.concatenate([slots_ref[s, rows, half] for s in range(SUBS)], axis=1)
        x_ref[i] = x
        if i < REACH:
            low_ref[i] = x
        if i >= LEAVES - REACH:
            high_ref[i - (LEAVES - REACH)] = x


def join_kernel(sub_ref, got0_ref, got1_ref, got2_ref, got3_ref, near_ref, basis_ref, slots_ref):
    in_order(sub_ref, [got0_ref, got1_ref, got2_ref, got3_ref], slots_ref, SENT)

    def whole(i, start, size):
        half = slice((i % 2) * ROWS, (i % 2 + 1) * ROWS)
        rows = pl.ds(start + (i // 2) * size, size)
        return jnp.concatenate([slots_ref[s, rows, half] for s in range(SUBS)], axis=1)

    for i in range(LEAVES):
        near_ref[i // 4, pl.ds(i % 4 * PROBES, PROBES), :] = whole(i, 0, PROBES)
        basis_ref[i // 4, pl.ds(i % 4 * RANK, RANK), :] = whole(i, PACKED, RANK)


def weights_kernel(_, couplings_ref, coarse_ref, out_ref):
    for q in range(PARENTS + 1):
        for c in range(4):
            for k in range(0, FAR, 2):
                ref, i = (couplings_ref, 4 * q + c) if q < PARENTS else (coarse_ref, c)
                n = (i * FAR + k) * RANK
                pair = [ref[n : n + RANK], ref[n + RANK : n + 2 * RANK]]
                both = jnp.concatenate(pair, axis=1)
                out_ref[q, pl.ds(c * RANK, RANK), pl.ds(k * RANK, LANES)] = both


def both_halves(row_pair):
    turned = pltpu.roll(row_pair, RANK, 1)
    left = lax.broadcasted_iota(jnp.int32, row_pair.shape, 1) < RANK
    return jnp.where(left, row_pair, turned), jnp.where(left, turned, row_pair)


def unpack_tile(tile, rows_ref, first):
    wide = tile.astype(F32)
    for h in range(2):
        one, two = both_halves(wide[h * OWN : (h + 1) * OWN])
        rows_ref[first + 2 * h] = one
        rows_ref[first + 2 * h + 1] = two


def choose_kernel(asked_ref, got_ref, out_ref, rows_ref):
    for z in range(PLANES):
        for t in range(LEAVES // 4):
            unpack_tile(got_ref[z, t], rows_ref, z * LEAVES + 4 * t)
    left = lax.broadcasted_iota(jnp.int32, (OWN, LANES), 1) < RANK
    for m in range(PLANE):
        for t in range(LEAF_OUT):
            rows = []
            for n in range(4 * t, 4 * t + 4):
                rows.append(rows_ref[n // CAP * LEAVES + asked_ref[m, n]])
            top = jnp.where(left, rows[0], rows[1])
            bottom = jnp.where(left, rows[2], rows[3])
            out_ref[m, t] = jnp.concatenate([top, bottom], axis=0).astype(BF16)
        for z in range(PLANES):
            out_ref[m, LEAF_OUT + z] = got_ref[z, TILES - 1]
        if m % 4 == 3:
            out_ref.send(m // 4)


def far_field(far_ref, coarse_ref, got_ref, weights_ref, transfer_ref, rows_ref):
    for n in range(PLANE * OUT_TILES):
        unpack_tile(got_ref[n], rows_ref, 4 * n)
    rows_ref[GOT_ROWS] = jnp.zeros((OWN, LANES), F32)
    left = lax.broadcasted_iota(jnp.int32, (OWN, LANES), 1) < RANK

    def apply(index_ref, q, weights):
        picked = []
        for c in range(4):
            pairs = []
            for k in range(0, FAR, 2):
                one = rows_ref[index_ref[4 * q + c, k]]
                two = rows_ref[index_ref[4 * q + c, k + 1]]
                pairs.append(jnp.where(left, one, two))
            picked.append(jnp.concatenate(pairs, axis=1))
        picked = jnp.concatenate(picked, axis=0).astype(BF16)
        return diagonal(dot_nt(picked, weights), OWN)

    coarse = apply(coarse_ref, 0, weights_ref[PARENTS]).astype(BF16)
    fields = []
    for q in range(PARENTS):
        down = dot_nt(coarse[:, q * RANK : (q + 1) * RANK], transfer_ref[q])
        fields.append(apply(far_ref, q, weights_ref[q]) + down)
    return fields


def field_kernel(
    far_ref, coarse_ref, got_ref, weights_ref, transfer_ref, out_ref, rows_ref
):
    fields = far_field(far_ref, coarse_ref, got_ref, weights_ref, transfer_ref, rows_ref)
    for q in range(PARENTS):
        out_ref[q] = to_tile(fields[q])


def field_of(field_ref, q):
    tiles = [field_ref[s, q].astype(F32) for s in range(SUBS)]
    field = [jnp.concatenate([t[:OWN], t[OWN:]], axis=1) for t in tiles]
    return spread_diagonal(jnp.concatenate(field, axis=0)).astype(BF16)


def second_kernel(
    sub_ref,
    field0_ref,
    field1_ref,
    field2_ref,
    field3_ref,
    near_ref,
    basis_ref,
    transfer_ref,
    x_ref,
    low_ref,
    high_ref,
    out_ref,
    field_ref,
    four_ref,
):
    in_order(sub_ref, [field0_ref, field1_ref, field2_ref, field3_ref], field_ref, PARENTS)
    own = probes_of(sub_ref[0])
    tiles = []
    parents = []
    for q in range(PARENTS):
        far = dot(field_of(field_ref, q), basis_ref[q])
        x = near_ref[q].astype(F32) + far
        mine = []
        for c in range(4):
            i = 4 * q + c
            four_ref[c] = x[c * PROBES : (c + 1) * PROBES]
            mine.append(four_ref[c, own, :])
            leaf = x[c * PROBES : (c + 1) * PROBES].astype(BF16)
            x_ref[i] = leaf
            if i < REACH:
                low_ref[i] = leaf
            if i >= LEAVES - REACH:
                high_ref[i - (LEAVES - REACH)] = leaf
        x_ref.send(q)
        mine = jnp.concatenate(mine, axis=0).astype(BF16)
        leaf = diagonal(dot_nt(mine, basis_ref[q]), OWN)
        tiles.append(to_tile(leaf))
        parents.append(dot(leaf.astype(BF16), transfer_ref[q]))
    tiles.append(to_tile(jnp.concatenate(parents, axis=1)))
    for t in range(TILES):
        for z in range(PLANES):
            out_ref[z, t] = tiles[t]


def output_kernel(
    sub_ref, field0_ref, field1_ref, field2_ref, field3_ref, near_ref, basis_ref, out_ref, field_ref
):
    in_order(sub_ref, [field0_ref, field1_ref, field2_ref, field3_ref], field_ref, PARENTS)
    outs = []
    for q in range(PARENTS):
        far = dot(field_of(field_ref, q), basis_ref[q])
        for c in range(4):
            outs.append(near_ref[4 * q + c] + far[c * PROBES : (c + 1) * PROBES])
    out_ref[...] = jnp.transpose(jnp.stack(outs), (1, 0, 2)).astype(BF16)


def near_parts(first_ref, list_ref, x_ref, low_ref, high_ref, blocks_ref, wide_ref):
    wide_ref[pl.ds(0, REACH)] = low_ref[...]
    wide_ref[pl.ds(REACH, LEAVES)] = x_ref[...]
    wide_ref[pl.ds(REACH + LEAVES, REACH)] = high_ref[...]
    wide_ref[2 * REACH + LEAVES] = jnp.zeros((PROBES, UNKNOWNS), BF16)

    def of_slot(i, k):
        leaf = list_ref[i, k]
        place = jnp.where(leaf >= 0, leaf - first_ref[0] + REACH, LEAVES + 2 * REACH)
        return wide_ref[place]

    for q in range(PARENTS):
        four = []
        for i in range(4 * q, 4 * q + 4):
            x = jnp.concatenate([of_slot(i, k) for k in range(NEAR)], axis=1)
            starts = [(i * NEAR + k) * ROWS for k in range(NEAR)]
            blocks = jnp.concatenate([blocks_ref[n : n + ROWS] for n in starts], axis=1)
            four.append(dot_nt(x, blocks))
        yield four


def near_sent_kernel(
    first_ref, list_ref, x_ref, low_ref, high_ref, blocks_ref, basis_ref, out_ref, wide_ref
):
    parts = near_parts(first_ref, list_ref, x_ref, low_ref, high_ref, blocks_ref, wide_ref)
    for q, four in enumerate(parts):
        for j in range(2):
            pair = jnp.concatenate(four[2 * j : 2 * j + 2], axis=1).astype(BF16)
            out_ref[pl.ds((2 * q + j) * PROBES, PROBES), :] = pair
    for j in range(LEAVES // 2):
        pair = jnp.concatenate([basis_ref[2 * j], basis_ref[2 * j + 1]], axis=1)
        out_ref[pl.ds(PACKED + j * RANK, RANK), :] = pair


def near_kernel(
    sub_ref, first_ref, list_ref, x_ref, low_ref, high_ref, blocks_ref, out_ref, mine_ref, wide_ref
):
    parts = near_parts(first_ref, list_ref, x_ref, low_ref, high_ref, blocks_ref, wide_ref)
    for q, four in enumerate(parts):
        for c in range(4):
            out_ref[4 * q + c] = four[c]
        out_ref.send(q)
    outs = []
    for i in range(LEAVES):
        x = x_ref[i].astype(F32)
        mine = x[:, :ROWS]
        for s in range(1, SUBS):
            mine = jnp.where(sub_ref[0] == s, x[:, s * ROWS : (s + 1) * ROWS], mine)
        outs.append(mine)
    mine_ref[...] = jnp.transpose(jnp.stack(outs), (1, 0, 2)).astype(BF16)


def local(
    probes,
    near_blocks,
    leaf_cluster_basis,
    transfer,
    couplings,
    coarse_couplings,
    near_list,
    distant_interaction_list,
    coarse_list,
):
    groups = PLANES * PLANE
    in_plane = [[z * PLANE + m for m in range(PLANE)] for z in range(PLANES)]
    along_z = [[z * PLANE + m for z in range(PLANES)] for m in range(PLANE)]
    sub = lax.axis_index("sub").reshape(1)
    first_leaf = (lax.axis_index("leaf") * LEAVES).reshape(1)
    four_transfers = transfer.reshape(PARENTS, BRANCH * RANK, RANK)
    four_bases = leaf_cluster_basis.reshape(PARENTS, BRANCH * RANK, ROWS)

    def over_sub(pieces):
        return [pieces[0]] + [
            lax.ppermute(pieces[k], "sub", [(i, (i + k) % SUBS) for i in range(SUBS)])
            for k in range(1, SUBS)
        ]

    x_shape = (LEAVES, PROBES, UNKNOWNS)
    edge = (REACH, PROBES, UNKNOWNS)
    tile = (16, LANES)
    message = (PLANES, TILES) + tile
    rows_scratch = [pltpu.VMEM((GOT_ROWS + 1, OWN, LANES), F32)]

    wide_scratch = [pltpu.VMEM((LEAVES + 2 * REACH + 1, PROBES, UNKNOWNS), BF16)]

    def halos(low, high):
        from_below = lax.ppermute(high, "leaf", [(i, i + 1) for i in range(groups - 1)])
        from_above = lax.ppermute(low, "leaf", [(i + 1, i) for i in range(groups - 1)])
        return from_below, from_above

    def near_args(x, from_below, from_above, where):
        tables = of_kind("smem", first_leaf) + of_kind("table", near_list)
        blocks = of_kind("cut", near_blocks.reshape(-1, UNKNOWNS))
        return tables + of_kind("hbm", x) + of_kind(where, from_below, from_above) + blocks

    def along(tiles):
        return lax.all_to_all(tiles, "leaf", 0, 0, axis_index_groups=along_z, tiled=True)

    def within(column, asked):
        (chosen,) = call(
            choose_kernel,
            "choose_rows",
            [((PLANE, OUT_TILES) + tile, BF16, 2)],
            of_kind("smem", asked) + of_kind("vmem", column),
            [pltpu.VMEM((PLANES * LEAVES, OWN, LANES), F32)],
        )
        got = lax.all_to_all(chosen, "leaf", 0, 0, axis_index_groups=in_plane, tiled=True)
        return got.reshape((PLANE * OUT_TILES,) + tile)

    packed = call(
        partial_kernel,
        "partial_sums",
        [((PACKED + TILES * 16, LANES), BF16)] * SUBS,
        of_kind("smem", sub) + of_kind("hbm", probes, four_bases, four_transfers),
        [pltpu.VMEM((TILES, PROBES, 4 * RANK), F32)],
    )
    first_leaf, packed = lax.optimization_barrier((first_leaf, packed))
    wanted, far_index, coarse_index = call(
        index_kernel,
        "index_tables",
        [
            ((PLANE, LANES), jnp.int32),
            (distant_interaction_list.shape, jnp.int32, 1),
            (coarse_list.shape, jnp.int32, 1),
        ],
        of_kind("smem", first_leaf) + of_kind("hbm", distant_interaction_list, coarse_list),
    )
    pieces, wanted = lax.optimization_barrier((over_sub(packed), wanted))
    x0, low, high, tiles = call(
        first_kernel,
        "first_coefficients",
        [(x_shape, BF16, 1), (edge, BF16), (edge, BF16), (message, BF16, 1)],
        of_kind("smem", sub) + of_kind("vmem", *pieces),
        [pltpu.VMEM((SUBS, PACKED, LANES), BF16)],
    )
    column, wanted = lax.optimization_barrier((along(tiles), wanted))
    asked = lax.all_to_all(wanted, "leaf", 0, 0, axis_index_groups=in_plane, tiled=True)
    (sent,) = call(
        near_sent_kernel,
        "near_field_sent",
        [((SENT, LANES), BF16, 1)],
        near_args(x0, *halos(low, high), "vmem") + of_kind("hbm", leaf_cluster_basis),
        wide_scratch,
    )
    column, sent, later = lax.optimization_barrier((column, sent, sub))
    got = within(column, asked)
    (weights,) = call(
        weights_kernel,
        "join_couplings",
        [((PARENTS + 1, 4 * RANK, FAR * RANK), BF16)],
        of_kind("smem", later) + of_kind("cut", couplings.reshape(-1, RANK), coarse_couplings.reshape(-1, RANK)),
    )

    def far(got):
        (field,) = call(
            field_kernel,
            "far_field",
            [((PARENTS,) + tile, BF16)],
            of_kind("table", far_index, coarse_index)
            + of_kind("vmem", got, weights, four_transfers),
            rows_scratch,
        )
        return field

    field_scratch = pltpu.VMEM((SUBS, PARENTS) + tile, BF16)
    field1, pieces = far(got), over_sub([sent] * SUBS)
    near1, basis = call(
        join_kernel,
        "join_near_basis",
        [((PARENTS, 4 * PROBES, UNKNOWNS), BF16), ((PARENTS, 4 * RANK, UNKNOWNS), BF16)],
        of_kind("smem", sub) + of_kind("hbm", pieces[0]) + of_kind("any", *pieces[1:]),
        [pltpu.VMEM((SUBS, SENT, LANES), BF16)],
    )
    x1, low, high, tiles = call(
        second_kernel,
        "second_coefficients",
        [(x_shape, BF16, 4), (edge, BF16), (edge, BF16), (message, BF16, 1)],
        of_kind("smem", sub)
        + of_kind("vmem", *over_sub([field1] * SUBS))
        + of_kind("vmem", near1, basis, four_transfers),
        [field_scratch, pltpu.VMEM((4, PROBES, UNKNOWNS), F32)],
    )
    column, edges = lax.optimization_barrier((along(tiles), halos(low, high)))
    got = within(column, asked)
    near2, first = call(
        near_kernel,
        "near_field",
        [((LEAVES, PROBES, ROWS), F32, 4), (probes.shape, BF16)],
        of_kind("smem", sub) + near_args(x1, *edges, "hbm"),
        wide_scratch,
    )
    got, near2 = lax.optimization_barrier((got, near2))
    (second_apply,) = call(
        output_kernel,
        "output",
        [(probes.shape, BF16)],
        of_kind("smem", sub)
        + of_kind("vmem", *over_sub([far(got)] * SUBS))
        + of_kind("hbm", near2)
        + of_kind("vmem", four_bases),
        [field_scratch],
    )
    return (first, second_apply)


def solution(mesh):
    return jax.shard_map(
        local,
        mesh=mesh,
        in_specs=(
            P(None, "leaf", "sub"),
            P("leaf", None, "sub", None),
            P("leaf", None, "sub"),
            P("leaf", None, None),
            P("leaf", None, None, None),
            P("leaf", None, None, None),
            P("leaf", None),
            P("leaf", None),
            P("leaf", None),
        ),
        out_specs=(P(None, "leaf", "sub"), P(None, "leaf", "sub")),
        check_vma=False,
    )
```

```python
import jax
import jax.numpy as jnp
from jax import lax
from jax.experimental import pallas as pl
from jax.experimental.pallas import tpu as pltpu
from jax.sharding import PartitionSpec as P

RANK = 64
BRANCH = 4
REACH = 4
CAP = 2
LEAVES = 16
PARENTS = 4
PROBES = 32
ROWS = 64
SUBS = 4
OWN = PROBES // SUBS
UNKNOWNS = SUBS * ROWS
NEAR = 9
FAR = 16
PLANES = 8
PLANE = 8
LANES = 128
TILES = PARENTS + 1
LEAF_OUT = PLANES * CAP // 4
OUT_TILES = LEAF_OUT + PLANES
GOT_ROWS = 4 * PLANE * OUT_TILES
PACKED = LEAVES // 2 * PROBES
PACKED_BASIS = LEAVES // 2 * RANK
BF16, F32 = jnp.bfloat16, jnp.float32

NT = (((1,), (1,)), ((), ()))
VMEM_LIMIT = 16 * 1024 * 1024


def dot(x, y):
    return jnp.dot(x, y, preferred_element_type=F32)


def dot_nt(x, y):
    return lax.dot_general(x, y, NT, preferred_element_type=F32)


class Arriving:
    def __init__(self, source, target, sems, parts):
        size = target.shape[0] // parts
        self.target, self.size, self.pending = target, size, {}
        for c in range(parts):
            part = pl.ds(c * size, size)
            copy = pltpu.make_async_copy(source.at[part], target.at[part], sems.at[c])
            copy.start()
            self.pending[c] = copy

    def finish(self, part=None):
        for c in list(self.pending) if part is None else [part]:
            if c in self.pending:
                self.pending.pop(c).wait()

    def __getitem__(self, index):
        first = index[0] if isinstance(index, tuple) else index
        if isinstance(first, slice) and first.start is not None:
            first = first.start
        self.finish(first // self.size if isinstance(first, int) else None)
        return self.target[index]


class Leaving:
    def __init__(self, source, target, sems, parts):
        size = target.shape[0] // parts
        self.source, self.started = source, []
        self.waiting = {}
        for c in range(parts):
            part = pl.ds(c * size, size)
            self.waiting[c] = pltpu.make_async_copy(source.at[part], target.at[part], sems.at[c])

    def __setitem__(self, index, value):
        self.source[index] = value

    def send(self, part=None):
        for c in list(self.waiting) if part is None else [part]:
            copy = self.waiting.pop(c)
            copy.start()
            self.started.append(copy)

    def finish(self):
        self.send()
        for copy in self.started:
            copy.wait()


PARTS = {"hbm": 1, "any": 1, "cut": 4}


def call(kernel, name, outs, args, scratch=()):
    spaces = {"smem": pltpu.SMEM, "table": pltpu.SMEM, "vmem": pltpu.VMEM, "any": pl.ANY}
    moved = [j for j, (kind, _) in enumerate(args) if kind in PARTS]
    away = [j for j, out in enumerate(outs) if len(out) == 3]
    scratch = list(scratch)
    buffers = [pltpu.VMEM(args[j][1].shape, args[j][1].dtype) for j in moved]
    buffers += [pltpu.VMEM(outs[j][0], outs[j][1]) for j in away]

    def body(*refs):
        refs = list(refs)
        sems = refs.pop()
        front = len(args) + len(outs) + len(scratch)
        used = 0
        for n, j in enumerate(moved):
            count = PARTS[args[j][0]]
            refs[j] = Arriving(refs[j], refs[front + n], sems.at[pl.ds(used, count)], count)
            used += count
        for n, j in enumerate(away):
            target, source = refs[len(args) + j], refs[front + len(moved) + n]
            count = outs[j][2]
            refs[len(args) + j] = Leaving(source, target, sems.at[pl.ds(used, count)], count)
            used += count
        kernel(*refs[:front])
        for ref in refs[:front]:
            if isinstance(ref, (Arriving, Leaving)):
                ref.finish()

    count = sum(PARTS[args[j][0]] for j in moved) + sum(outs[j][2] for j in away)
    return pl.pallas_call(
        body,
        name=name,
        out_shape=[
            pltpu.HBM(out[0], out[1]) if len(out) == 3 else jax.ShapeDtypeStruct(*out) for out in outs
        ],
        in_specs=[pl.BlockSpec(memory_space=spaces.get(kind, pltpu.HBM)) for kind, _ in args],
        out_specs=[
            pl.BlockSpec(memory_space=pltpu.HBM if j in away else pltpu.VMEM) for j in range(len(outs))
        ],
        scratch_shapes=scratch + buffers + [pltpu.SemaphoreType.DMA((max(count, 1),))],
        compiler_params=pltpu.CompilerParams(vmem_limit_bytes=VMEM_LIMIT),
    )(*[
        array if kind in ("smem", "vmem", "any") else pltpu.with_memory_space_constraint(array, pltpu.HBM)
        for kind, array in args
    ])


def of_kind(kind, *arrays):
    return [(kind, array) for array in arrays]


def lane_block(rows, lanes):
    return lax.broadcasted_iota(jnp.int32, (rows, lanes), 1) // RANK


def diagonal(x, rows):
    block = lane_block(rows, 4 * RANK)
    out = x[:rows]
    for c in range(1, 4):
        out = jnp.where(block == c, x[c * rows : (c + 1) * rows], out)
    return out


def spread_diagonal(x):
    block = lane_block(x.shape[0], 4 * RANK)
    return jnp.concatenate([jnp.where(block == c, x, jnp.zeros_like(x)) for c in range(4)], axis=0)


def to_tile(x):
    return jnp.concatenate([x[:, :LANES], x[:, LANES:]], axis=0).astype(BF16)


def index_kernel(_, far_ref, coarse_ref, wanted_ref, far_out_ref, coarse_out_ref):
    groups = PLANES * PLANE
    group = lax.broadcasted_iota(jnp.int32, (groups, FAR), 0)
    named = far_ref[...]
    owner = jnp.where(named >= 0, named >> 4, -1)
    place = (named & (LEAVES - 1)).astype(F32)
    hits = [owner[i : i + 1] == group for i in range(LEAVES)]
    least = jnp.full((groups, FAR), LEAVES - 1.0, F32)
    greatest = jnp.zeros((groups, FAR), F32)
    for i in range(LEAVES):
        least = jnp.minimum(least, jnp.where(hits[i], place[i : i + 1], LEAVES - 1.0))
        greatest = jnp.maximum(greatest, jnp.where(hits[i], place[i : i + 1], 0.0))
    least = jnp.min(least, axis=1, keepdims=True)
    greatest = jnp.max(greatest, axis=1, keepdims=True)
    lane = lax.broadcasted_iota(jnp.int32, (PLANE, LANES), 1)
    wanted = jnp.zeros((PLANE, LANES), F32)
    for z in range(PLANES):
        wanted = jnp.where(lane == CAP * z, least[z * PLANE : (z + 1) * PLANE], wanted)
        wanted = jnp.where(lane == CAP * z + 1, greatest[z * PLANE : (z + 1) * PLANE], wanted)
    wanted_ref[...] = wanted.astype(jnp.int32)
    of_entry = [
        jnp.sum(jnp.where(hits[i], least, 0.0), axis=0, keepdims=True) for i in range(LEAVES)
    ]
    second = jnp.where(place == jnp.concatenate(of_entry, axis=0), 0, 1)
    row = (owner & (PLANE - 1)) * (4 * OUT_TILES) + (owner >> 3) * CAP + second
    far_out_ref[...] = jnp.where(named >= 0, row, GOT_ROWS)
    coarse = coarse_ref[...]
    owner = coarse >> 2
    row = (owner & (PLANE - 1)) * (4 * OUT_TILES) + 4 * LEAF_OUT + (owner >> 3) * PARENTS
    coarse_out_ref[...] = jnp.where(coarse >= 0, row + (coarse & (PARENTS - 1)), GOT_ROWS)


def partial_kernel(
    sub_ref, x_ref, basis_ref, transfer_ref, out0_ref, out1_ref, out2_ref, out3_ref, packed_ref, sums_ref
):
    out_refs = [out0_ref, out1_ref, out2_ref, out3_ref]
    x = jnp.transpose(x_ref[...].astype(F32), (1, 0, 2)).astype(BF16)
    for j in range(LEAVES // 2):
        pair = jnp.concatenate([x[2 * j], x[2 * j + 1]], axis=1)
        for out_ref in out_refs:
            out_ref[pl.ds(j * PROBES, PROBES), :] = pair
        q, n = j // 2, j % 2 * 2 * RANK
        pair = [basis_ref[q, n : n + RANK, :], basis_ref[q, n + RANK : n + 2 * RANK, :]]
        packed_ref[pl.ds(j * RANK, RANK), :] = jnp.concatenate(pair, axis=1)
    packed_ref.send()
    parents = []
    sums = []
    for q in range(PARENTS):
        four = x[4 * q : 4 * q + 4].reshape(4 * PROBES, ROWS)
        leaf = diagonal(dot_nt(four, basis_ref[q]), PROBES)
        sums.append(leaf)
        parents.append(dot(leaf.astype(BF16), transfer_ref[q]))
    sums.append(jnp.concatenate(parents, axis=1))
    for t in range(TILES):
        sums_ref[t] = sums[t]
    for k, out_ref in enumerate(out_refs):
        place = probes_of((sub_ref[0] + k) % SUBS)
        for t in range(TILES):
            out_ref[pl.ds(PACKED + 16 * t, 16), :] = to_tile(sums_ref[t, place, :])


def probes_of(sub):
    return pl.ds(pl.multiple_of(sub * OWN, OWN), OWN)


def in_order(sub_ref, piece_refs, slots_ref, rows):
    for k, piece_ref in enumerate(piece_refs):
        slots_ref[(sub_ref[0] + SUBS - k) % SUBS] = piece_ref[pl.ds(0, rows)]


def first_kernel(
    sub_ref, got0_ref, got1_ref, got2_ref, got3_ref, x_ref, low_ref, high_ref, out_ref, slots_ref
):
    got_refs = [got0_ref, got1_ref, got2_ref, got3_ref]
    for t in range(TILES):
        total = got0_ref[pl.ds(PACKED + 16 * t, 16), :].astype(F32)
        for got_ref in got_refs[1:]:
            total = total + got_ref[pl.ds(PACKED + 16 * t, 16), :].astype(F32)
        tile = total.astype(BF16)
        for z in range(PLANES):
            out_ref[z, t] = tile
    out_ref.send()
    in_order(sub_ref, got_refs, slots_ref, PACKED)
    for i in range(LEAVES):
        half = slice((i % 2) * ROWS, (i % 2 + 1) * ROWS)
        rows = pl.ds((i // 2) * PROBES, PROBES)
        x = jnp.concatenate([slots_ref[s, rows, half] for s in range(SUBS)], axis=1)
        x_ref[i] = x
        if i < REACH:
            low_ref[i] = x
        if i >= LEAVES - REACH:
            high_ref[i - (LEAVES - REACH)] = x


def join_kernel(
    sub_ref,
    near0_ref,
    near1_ref,
    near2_ref,
    near3_ref,
    basis0_ref,
    basis1_ref,
    basis2_ref,
    basis3_ref,
    near_ref,
    basis_ref,
    near_slots_ref,
    basis_slots_ref,
):
    basis_refs = [basis0_ref, basis1_ref, basis2_ref, basis3_ref]
    in_order(sub_ref, basis_refs, basis_slots_ref, PACKED_BASIS)
    in_order(sub_ref, [near0_ref, near1_ref, near2_ref, near3_ref], near_slots_ref, PACKED)

    def whole(slots_ref, i, size):
        half = slice((i % 2) * ROWS, (i % 2 + 1) * ROWS)
        rows = pl.ds((i // 2) * size, size)
        return jnp.concatenate([slots_ref[s, rows, half] for s in range(SUBS)], axis=1)

    for i in range(LEAVES):
        near_ref[i // 4, pl.ds(i % 4 * PROBES, PROBES), :] = whole(near_slots_ref, i, PROBES)
        basis_ref[i // 4, pl.ds(i % 4 * RANK, RANK), :] = whole(basis_slots_ref, i, RANK)


def weights_kernel(_, couplings_ref, coarse_ref, out_ref):
    for q in range(PARENTS + 1):
        for c in range(4):
            for k in range(0, FAR, 2):
                ref, i = (couplings_ref, 4 * q + c) if q < PARENTS else (coarse_ref, c)
                n = (i * FAR + k) * RANK
                pair = [ref[n : n + RANK], ref[n + RANK : n + 2 * RANK]]
                both = jnp.concatenate(pair, axis=1)
                out_ref[q, pl.ds(c * RANK, RANK), pl.ds(k * RANK, LANES)] = both


def both_halves(row_pair):
    turned = pltpu.roll(row_pair, RANK, 1)
    left = lax.broadcasted_iota(jnp.int32, row_pair.shape, 1) < RANK
    return jnp.where(left, row_pair, turned), jnp.where(left, turned, row_pair)


def unpack_tile(tile, rows_ref, first):
    wide = tile.astype(F32)
    for h in range(2):
        one, two = both_halves(wide[h * OWN : (h + 1) * OWN])
        rows_ref[first + 2 * h] = one
        rows_ref[first + 2 * h + 1] = two


def choose_kernel(asked_ref, got_ref, out_ref, rows_ref):
    for z in range(PLANES):
        for t in range(LEAVES // 4):
            unpack_tile(got_ref[z, t], rows_ref, z * LEAVES + 4 * t)
    left = lax.broadcasted_iota(jnp.int32, (OWN, LANES), 1) < RANK
    for m in range(PLANE):
        for t in range(LEAF_OUT):
            rows = []
            for n in range(4 * t, 4 * t + 4):
                rows.append(rows_ref[n // CAP * LEAVES + asked_ref[m, n]])
            top = jnp.where(left, rows[0], rows[1])
            bottom = jnp.where(left, rows[2], rows[3])
            out_ref[m, t] = jnp.concatenate([top, bottom], axis=0).astype(BF16)
        for z in range(PLANES):
            out_ref[m, LEAF_OUT + z] = got_ref[z, TILES - 1]
        if m % 4 == 3:
            out_ref.send(m // 4)


def far_field(far_ref, coarse_ref, got_ref, weights_ref, transfer_ref, rows_ref):
    for n in range(PLANE * OUT_TILES):
        unpack_tile(got_ref[n], rows_ref, 4 * n)
    rows_ref[GOT_ROWS] = jnp.zeros((OWN, LANES), F32)
    left = lax.broadcasted_iota(jnp.int32, (OWN, LANES), 1) < RANK

    def apply(index_ref, q, weights):
        picked = []
        for c in range(4):
            pairs = []
            for k in range(0, FAR, 2):
                one = rows_ref[index_ref[4 * q + c, k]]
                two = rows_ref[index_ref[4 * q + c, k + 1]]
                pairs.append(jnp.where(left, one, two))
            picked.append(jnp.concatenate(pairs, axis=1))
        picked = jnp.concatenate(picked, axis=0).astype(BF16)
        return diagonal(dot_nt(picked, weights), OWN)

    coarse = apply(coarse_ref, 0, weights_ref[PARENTS]).astype(BF16)
    fields = []
    for q in range(PARENTS):
        down = dot_nt(coarse[:, q * RANK : (q + 1) * RANK], transfer_ref[q])
        fields.append(apply(far_ref, q, weights_ref[q]) + down)
    return fields


def field_kernel(
    far_ref, coarse_ref, got_ref, weights_ref, transfer_ref, out_ref, rows_ref
):
    fields = far_field(far_ref, coarse_ref, got_ref, weights_ref, transfer_ref, rows_ref)
    for q in range(PARENTS):
        out_ref[q] = to_tile(fields[q])


def field_of(field_ref, q):
    tiles = [field_ref[s, q].astype(F32) for s in range(SUBS)]
    field = [jnp.concatenate([t[:OWN], t[OWN:]], axis=1) for t in tiles]
    return spread_diagonal(jnp.concatenate(field, axis=0)).astype(BF16)


def second_kernel(
    sub_ref,
    field0_ref,
    field1_ref,
    field2_ref,
    field3_ref,
    near_ref,
    basis_ref,
    transfer_ref,
    x_ref,
    low_ref,
    high_ref,
    out_ref,
    field_ref,
    four_ref,
):
    in_order(sub_ref, [field0_ref, field1_ref, field2_ref, field3_ref], field_ref, PARENTS)
    own = probes_of(sub_ref[0])
    tiles = []
    parents = []
    for q in range(PARENTS):
        far = dot(field_of(field_ref, q), basis_ref[q])
        x = near_ref[q].astype(F32) + far
        mine = []
        for c in range(4):
            i = 4 * q + c
            four_ref[c] = x[c * PROBES : (c + 1) * PROBES]
            mine.append(four_ref[c, own, :])
            leaf = x[c * PROBES : (c + 1) * PROBES].astype(BF16)
            x_ref[i] = leaf
            if i < REACH:
                low_ref[i] = leaf
            if i >= LEAVES - REACH:
                high_ref[i - (LEAVES - REACH)] = leaf
        x_ref.send(q)
        mine = jnp.concatenate(mine, axis=0).astype(BF16)
        leaf = diagonal(dot_nt(mine, basis_ref[q]), OWN)
        tiles.append(to_tile(leaf))
        parents.append(dot(leaf.astype(BF16), transfer_ref[q]))
    tiles.append(to_tile(jnp.concatenate(parents, axis=1)))
    for t in range(TILES):
        for z in range(PLANES):
            out_ref[z, t] = tiles[t]


def output_kernel(
    sub_ref, field0_ref, field1_ref, field2_ref, field3_ref, near_ref, basis_ref, out_ref, field_ref
):
    in_order(sub_ref, [field0_ref, field1_ref, field2_ref, field3_ref], field_ref, PARENTS)
    outs = []
    for q in range(PARENTS):
        far = dot(field_of(field_ref, q), basis_ref[q])
        for c in range(4):
            outs.append(near_ref[4 * q + c] + far[c * PROBES : (c + 1) * PROBES])
    out_ref[...] = jnp.transpose(jnp.stack(outs), (1, 0, 2)).astype(BF16)


def near_parts(first_ref, list_ref, x_ref, low_ref, high_ref, blocks_ref, wide_ref):
    wide_ref[pl.ds(0, REACH)] = low_ref[...]
    wide_ref[pl.ds(REACH, LEAVES)] = x_ref[...]
    wide_ref[pl.ds(REACH + LEAVES, REACH)] = high_ref[...]
    wide_ref[2 * REACH + LEAVES] = jnp.zeros((PROBES, UNKNOWNS), BF16)

    def of_slot(i, k):
        leaf = list_ref[i, k]
        place = jnp.where(leaf >= 0, leaf - first_ref[0] + REACH, LEAVES + 2 * REACH)
        return wide_ref[place]

    for q in range(PARENTS):
        four = []
        for i in range(4 * q, 4 * q + 4):
            x = jnp.concatenate([of_slot(i, k) for k in range(NEAR)], axis=1)
            starts = [(i * NEAR + k) * ROWS for k in range(NEAR)]
            blocks = jnp.concatenate([blocks_ref[n : n + ROWS] for n in starts], axis=1)
            four.append(dot_nt(x, blocks))
        yield four


def near_sent_kernel(
    first_ref, list_ref, x_ref, low_ref, high_ref, blocks_ref, out_ref, wide_ref
):
    parts = near_parts(first_ref, list_ref, x_ref, low_ref, high_ref, blocks_ref, wide_ref)
    for q, four in enumerate(parts):
        for j in range(2):
            pair = jnp.concatenate(four[2 * j : 2 * j + 2], axis=1).astype(BF16)
            out_ref[pl.ds((2 * q + j) * PROBES, PROBES), :] = pair


def near_kernel(
    sub_ref, first_ref, list_ref, x_ref, low_ref, high_ref, blocks_ref, out_ref, mine_ref, wide_ref
):
    parts = near_parts(first_ref, list_ref, x_ref, low_ref, high_ref, blocks_ref, wide_ref)
    for q, four in enumerate(parts):
        for c in range(4):
            out_ref[4 * q + c] = four[c]
        out_ref.send(q)
    outs = []
    for i in range(LEAVES):
        x = x_ref[i].astype(F32)
        mine = x[:, :ROWS]
        for s in range(1, SUBS):
            mine = jnp.where(sub_ref[0] == s, x[:, s * ROWS : (s + 1) * ROWS], mine)
        outs.append(mine)
    mine_ref[...] = jnp.transpose(jnp.stack(outs), (1, 0, 2)).astype(BF16)


def local(
    probes,
    near_blocks,
    leaf_cluster_basis,
    transfer,
    couplings,
    coarse_couplings,
    near_list,
    distant_interaction_list,
    coarse_list,
):
    groups = PLANES * PLANE
    in_plane = [[z * PLANE + m for m in range(PLANE)] for z in range(PLANES)]
    along_z = [[z * PLANE + m for z in range(PLANES)] for m in range(PLANE)]
    sub = lax.axis_index("sub").reshape(1)
    first_leaf = (lax.axis_index("leaf") * LEAVES).reshape(1)
    four_transfers = transfer.reshape(PARENTS, BRANCH * RANK, RANK)
    four_bases = leaf_cluster_basis.reshape(PARENTS, BRANCH * RANK, ROWS)

    def over_sub(pieces):
        return [pieces[0]] + [
            lax.ppermute(pieces[k], "sub", [(i, (i + k) % SUBS) for i in range(SUBS)])
            for k in range(1, SUBS)
        ]

    x_shape = (LEAVES, PROBES, UNKNOWNS)
    edge = (REACH, PROBES, UNKNOWNS)
    tile = (16, LANES)
    message = (PLANES, TILES) + tile
    rows_scratch = [pltpu.VMEM((GOT_ROWS + 1, OWN, LANES), F32)]

    wide_scratch = [pltpu.VMEM((LEAVES + 2 * REACH + 1, PROBES, UNKNOWNS), BF16)]

    def halos(low, high):
        from_below = lax.ppermute(high, "leaf", [(i, i + 1) for i in range(groups - 1)])
        from_above = lax.ppermute(low, "leaf", [(i + 1, i) for i in range(groups - 1)])
        return from_below, from_above

    def near_args(x, from_below, from_above, where):
        tables = of_kind("smem", first_leaf) + of_kind("table", near_list)
        blocks = of_kind("cut", near_blocks.reshape(-1, UNKNOWNS))
        return tables + of_kind("hbm", x) + of_kind(where, from_below, from_above) + blocks

    def along(tiles):
        return lax.all_to_all(tiles, "leaf", 0, 0, axis_index_groups=along_z, tiled=True)

    def within(column, asked, edges=()):
        (chosen,) = call(
            choose_kernel,
            "choose_rows",
            [((PLANE, OUT_TILES) + tile, BF16, 2)],
            of_kind("smem", asked) + of_kind("vmem", column),
            [pltpu.VMEM((PLANES * LEAVES, OWN, LANES), F32)],
        )
        chosen, edges = lax.optimization_barrier((chosen, edges))
        got = lax.all_to_all(chosen, "leaf", 0, 0, axis_index_groups=in_plane, tiled=True)
        return got.reshape((PLANE * OUT_TILES,) + tile), edges

    *packed, packed_basis = call(
        partial_kernel,
        "partial_sums",
        [((PACKED + TILES * 16, LANES), BF16)] * SUBS + [((PACKED_BASIS, LANES), BF16, 1)],
        of_kind("smem", sub) + of_kind("hbm", probes, four_bases, four_transfers),
        [pltpu.VMEM((TILES, PROBES, 4 * RANK), F32)],
    )
    first_leaf, packed = lax.optimization_barrier((first_leaf, packed))
    wanted, far_index, coarse_index = call(
        index_kernel,
        "index_tables",
        [
            ((PLANE, LANES), jnp.int32),
            (distant_interaction_list.shape, jnp.int32, 1),
            (coarse_list.shape, jnp.int32, 1),
        ],
        of_kind("smem", first_leaf) + of_kind("hbm", distant_interaction_list, coarse_list),
    )
    pieces, wanted = lax.optimization_barrier((over_sub(packed), wanted))
    x0, low, high, tiles = call(
        first_kernel,
        "first_coefficients",
        [(x_shape, BF16, 1), (edge, BF16), (edge, BF16), (message, BF16, 1)],
        of_kind("smem", sub) + of_kind("vmem", *pieces),
        [pltpu.VMEM((SUBS, PACKED, LANES), BF16)],
    )
    bases = over_sub([packed_basis] * SUBS)
    column, wanted, bases = lax.optimization_barrier((along(tiles), wanted, bases))
    asked = lax.all_to_all(wanted, "leaf", 0, 0, axis_index_groups=in_plane, tiled=True)
    (sent,) = call(
        near_sent_kernel,
        "near_field_sent",
        [((PACKED, LANES), BF16, 1)],
        near_args(x0, *halos(low, high), "vmem"),
        wide_scratch,
    )
    column, sent, later = lax.optimization_barrier((column, sent, sub))
    got, _ = within(column, asked)
    (weights,) = call(
        weights_kernel,
        "join_couplings",
        [((PARENTS + 1, 4 * RANK, FAR * RANK), BF16)],
        of_kind("smem", later) + of_kind("cut", couplings.reshape(-1, RANK), coarse_couplings.reshape(-1, RANK)),
    )

    def far(got):
        (field,) = call(
            field_kernel,
            "far_field",
            [((PARENTS,) + tile, BF16)],
            of_kind("table", far_index, coarse_index)
            + of_kind("vmem", got, weights, four_transfers),
            rows_scratch,
        )
        return field

    field_scratch = pltpu.VMEM((SUBS, PARENTS) + tile, BF16)
    field1, pieces = far(got), over_sub([sent] * SUBS)
    near1, basis = call(
        join_kernel,
        "join_near_basis",
        [((PARENTS, 4 * PROBES, UNKNOWNS), BF16), ((PARENTS, 4 * RANK, UNKNOWNS), BF16)],
        of_kind("smem", sub)
        + of_kind("hbm", pieces[0])
        + of_kind("any", *pieces[1:])
        + of_kind("hbm", *bases),
        [pltpu.VMEM((SUBS, PACKED, LANES), BF16), pltpu.VMEM((SUBS, PACKED_BASIS, LANES), BF16)],
    )
    x1, low, high, tiles = call(
        second_kernel,
        "second_coefficients",
        [(x_shape, BF16, 4), (edge, BF16), (edge, BF16), (message, BF16, 1)],
        of_kind("smem", sub)
        + of_kind("vmem", *over_sub([field1] * SUBS))
        + of_kind("vmem", near1, basis, four_transfers),
        [field_scratch, pltpu.VMEM((4, PROBES, UNKNOWNS), F32)],
    )
    got, edges = within(along(tiles), asked, halos(low, high))
    near2, first = call(
        near_kernel,
        "near_field",
        [((LEAVES, PROBES, ROWS), F32, 4), (probes.shape, BF16)],
        of_kind("smem", sub) + near_args(x1, *edges, "hbm"),
        wide_scratch,
    )
    got, near2 = lax.optimization_barrier((got, near2))
    (second_apply,) = call(
        output_kernel,
        "output",
        [(probes.shape, BF16)],
        of_kind("smem", sub)
        + of_kind("vmem", *over_sub([far(got)] * SUBS))
        + of_kind("hbm", near2)
        + of_kind("vmem", four_bases),
        [field_scratch],
    )
    return (first, second_apply)


def solution(mesh):
    return jax.shard_map(
        local,
        mesh=mesh,
        in_specs=(
            P(None, "leaf", "sub"),
            P("leaf", None, "sub", None),
            P("leaf", None, "sub"),
            P("leaf", None, None),
            P("leaf", None, None, None),
            P("leaf", None, None, None),
            P("leaf", None),
            P("leaf", None),
            P("leaf", None),
        ),
        out_specs=(P(None, "leaf", "sub"), P(None, "leaf", "sub")),
        check_vma=False,
    )
```

```python
import jax
import jax.numpy as jnp
from jax import lax
from jax.experimental import pallas as pl
from jax.experimental.pallas import tpu as pltpu
from jax.sharding import PartitionSpec as P

RANK = 64
BRANCH = 4
REACH = 4
CAP = 2
LEAVES = 16
PARENTS = 4
PROBES = 32
ROWS = 64
SUBS = 4
OWN = PROBES // SUBS
UNKNOWNS = SUBS * ROWS
NEAR = 9
FAR = 16
PLANES = 8
PLANE = 8
LANES = 128
TILES = PARENTS + 1
LEAF_OUT = PLANES * CAP // 4
OUT_TILES = LEAF_OUT + PLANES
GOT_ROWS = 4 * PLANE * OUT_TILES
PACKED = LEAVES // 2 * PROBES
SENT = PACKED + LEAVES // 2 * RANK
BF16, F32 = jnp.bfloat16, jnp.float32

NT = (((1,), (1,)), ((), ()))
VMEM_LIMIT = 16 * 1024 * 1024


def dot(x, y):
    return jnp.dot(x, y, preferred_element_type=F32)


def dot_nt(x, y):
    return lax.dot_general(x, y, NT, preferred_element_type=F32)


class Arriving:
    def __init__(self, source, target, sems, parts):
        size = target.shape[0] // parts
        self.target, self.size, self.pending = target, size, {}
        for c in range(parts):
            part = pl.ds(c * size, size)
            copy = pltpu.make_async_copy(source.at[part], target.at[part], sems.at[c])
            copy.start()
            self.pending[c] = copy

    def finish(self, part=None):
        for c in list(self.pending) if part is None else [part]:
            if c in self.pending:
                self.pending.pop(c).wait()

    def __getitem__(self, index):
        first = index[0] if isinstance(index, tuple) else index
        if isinstance(first, slice) and first.start is not None:
            first = first.start
        self.finish(first // self.size if isinstance(first, int) else None)
        return self.target[index]


class Leaving:
    def __init__(self, source, target, sems, parts):
        size = target.shape[0] // parts
        self.source, self.started = source, []
        self.waiting = {}
        for c in range(parts):
            part = pl.ds(c * size, size)
            self.waiting[c] = pltpu.make_async_copy(source.at[part], target.at[part], sems.at[c])

    def __setitem__(self, index, value):
        self.source[index] = value

    def send(self, part=None):
        for c in list(self.waiting) if part is None else [part]:
            copy = self.waiting.pop(c)
            copy.start()
            self.started.append(copy)

    def finish(self):
        self.send()
        for copy in self.started:
            copy.wait()


PARTS = {"hbm": 1, "any": 1, "cut": 4}


def call(kernel, name, outs, args, scratch=()):
    spaces = {"smem": pltpu.SMEM, "table": pltpu.SMEM, "vmem": pltpu.VMEM, "any": pl.ANY}
    moved = [j for j, (kind, _) in enumerate(args) if kind in PARTS]
    away = [j for j, out in enumerate(outs) if len(out) == 3]
    scratch = list(scratch)
    buffers = [pltpu.VMEM(args[j][1].shape, args[j][1].dtype) for j in moved]
    buffers += [pltpu.VMEM(outs[j][0], outs[j][1]) for j in away]

    def body(*refs):
        refs = list(refs)
        sems = refs.pop()
        front = len(args) + len(outs) + len(scratch)
        used = 0
        for n, j in enumerate(moved):
            count = PARTS[args[j][0]]
            refs[j] = Arriving(refs[j], refs[front + n], sems.at[pl.ds(used, count)], count)
            used += count
        for n, j in enumerate(away):
            target, source = refs[len(args) + j], refs[front + len(moved) + n]
            count = outs[j][2]
            refs[len(args) + j] = Leaving(source, target, sems.at[pl.ds(used, count)], count)
            used += count
        kernel(*refs[:front])
        for ref in refs[:front]:
            if isinstance(ref, (Arriving, Leaving)):
                ref.finish()

    count = sum(PARTS[args[j][0]] for j in moved) + sum(outs[j][2] for j in away)
    return pl.pallas_call(
        body,
        name=name,
        out_shape=[
            pltpu.HBM(out[0], out[1]) if len(out) == 3 else jax.ShapeDtypeStruct(*out) for out in outs
        ],
        in_specs=[pl.BlockSpec(memory_space=spaces.get(kind, pltpu.HBM)) for kind, _ in args],
        out_specs=[
            pl.BlockSpec(memory_space=pltpu.HBM if j in away else pltpu.VMEM) for j in range(len(outs))
        ],
        scratch_shapes=scratch + buffers + [pltpu.SemaphoreType.DMA((max(count, 1),))],
        compiler_params=pltpu.CompilerParams(vmem_limit_bytes=VMEM_LIMIT),
    )(*[
        array if kind in ("smem", "vmem", "any") else pltpu.with_memory_space_constraint(array, pltpu.HBM)
        for kind, array in args
    ])


def of_kind(kind, *arrays):
    return [(kind, array) for array in arrays]


def lane_block(rows, lanes):
    return lax.broadcasted_iota(jnp.int32, (rows, lanes), 1) // RANK


def diagonal(x, rows):
    block = lane_block(rows, 4 * RANK)
    out = x[:rows]
    for c in range(1, 4):
        out = jnp.where(block == c, x[c * rows : (c + 1) * rows], out)
    return out


def spread_diagonal(x):
    block = lane_block(x.shape[0], 4 * RANK)
    return jnp.concatenate([jnp.where(block == c, x, jnp.zeros_like(x)) for c in range(4)], axis=0)


def to_tile(x):
    return jnp.concatenate([x[:, :LANES], x[:, LANES:]], axis=0).astype(BF16)


def index_kernel(_, far_ref, coarse_ref, wanted_ref, far_out_ref, coarse_out_ref):
    groups = PLANES * PLANE
    group = lax.broadcasted_iota(jnp.int32, (groups, FAR), 0)
    named = far_ref[...]
    owner = jnp.where(named >= 0, named >> 4, -1)
    place = (named & (LEAVES - 1)).astype(F32)
    hits = [owner[i : i + 1] == group for i in range(LEAVES)]
    least = jnp.full((groups, FAR), LEAVES - 1.0, F32)
    greatest = jnp.zeros((groups, FAR), F32)
    for i in range(LEAVES):
        least = jnp.minimum(least, jnp.where(hits[i], place[i : i + 1], LEAVES - 1.0))
        greatest = jnp.maximum(greatest, jnp.where(hits[i], place[i : i + 1], 0.0))
    least = jnp.min(least, axis=1, keepdims=True)
    greatest = jnp.max(greatest, axis=1, keepdims=True)
    lane = lax.broadcasted_iota(jnp.int32, (PLANE, LANES), 1)
    wanted = jnp.zeros((PLANE, LANES), F32)
    for z in range(PLANES):
        wanted = jnp.where(lane == CAP * z, least[z * PLANE : (z + 1) * PLANE], wanted)
        wanted = jnp.where(lane == CAP * z + 1, greatest[z * PLANE : (z + 1) * PLANE], wanted)
    wanted_ref[...] = wanted.astype(jnp.int32)
    of_entry = [
        jnp.sum(jnp.where(hits[i], least, 0.0), axis=0, keepdims=True) for i in range(LEAVES)
    ]
    second = jnp.where(place == jnp.concatenate(of_entry, axis=0), 0, 1)
    row = (owner & (PLANE - 1)) * (4 * OUT_TILES) + (owner >> 3) * CAP + second
    far_out_ref[...] = jnp.where(named >= 0, row, GOT_ROWS)
    coarse = coarse_ref[...]
    owner = coarse >> 2
    row = (owner & (PLANE - 1)) * (4 * OUT_TILES) + 4 * LEAF_OUT + (owner >> 3) * PARENTS
    coarse_out_ref[...] = jnp.where(coarse >= 0, row + (coarse & (PARENTS - 1)), GOT_ROWS)


def partial_kernel(
    sub_ref, x_ref, basis_ref, transfer_ref, out0_ref, out1_ref, out2_ref, out3_ref, sums_ref
):
    out_refs = [out0_ref, out1_ref, out2_ref, out3_ref]
    x = jnp.transpose(x_ref[...].astype(F32), (1, 0, 2)).astype(BF16)
    for j in range(LEAVES // 2):
        pair = jnp.concatenate([x[2 * j], x[2 * j + 1]], axis=1)
        for out_ref in out_refs:
            out_ref[pl.ds(j * PROBES, PROBES), :] = pair
    parents = []
    sums = []
    for q in range(PARENTS):
        four = x[4 * q : 4 * q + 4].reshape(4 * PROBES, ROWS)
        leaf = diagonal(dot_nt(four, basis_ref[q]), PROBES)
        sums.append(leaf)
        parents.append(dot(leaf.astype(BF16), transfer_ref[q]))
    sums.append(jnp.concatenate(parents, axis=1))
    for t in range(TILES):
        sums_ref[t] = sums[t]
    for k, out_ref in enumerate(out_refs):
        place = probes_of((sub_ref[0] + k) % SUBS)
        for t in range(TILES):
            out_ref[pl.ds(PACKED + 16 * t, 16), :] = to_tile(sums_ref[t, place, :])


def probes_of(sub):
    return pl.ds(pl.multiple_of(sub * OWN, OWN), OWN)


def in_order(sub_ref, piece_refs, slots_ref, rows):
    for k, piece_ref in enumerate(piece_refs):
        slots_ref[(sub_ref[0] + SUBS - k) % SUBS] = piece_ref[pl.ds(0, rows)]


def first_kernel(
    sub_ref, got0_ref, got1_ref, got2_ref, got3_ref, x_ref, low_ref, high_ref, out_ref, slots_ref
):
    got_refs = [got0_ref, got1_ref, got2_ref, got3_ref]
    for t in range(TILES):
        total = got0_ref[pl.ds(PACKED + 16 * t, 16), :].astype(F32)
        for got_ref in got_refs[1:]:
            total = total + got_ref[pl.ds(PACKED + 16 * t, 16), :].astype(F32)
        tile = total.astype(BF16)
        for z in range(PLANES):
            out_ref[z, t] = tile
    out_ref.send()
    in_order(sub_ref, got_refs, slots_ref, PACKED)
    for i in range(LEAVES):
        half = slice((i % 2) * ROWS, (i % 2 + 1) * ROWS)
        rows = pl.ds((i // 2) * PROBES, PROBES)
        x = jnp.concatenate([slots_ref[s, rows, half] for s in range(SUBS)], axis=1)
        x_ref[i] = x
        if i < REACH:
            low_ref[i] = x
        if i >= LEAVES - REACH:
            high_ref[i - (LEAVES - REACH)] = x


def join_kernel(sub_ref, got0_ref, got1_ref, got2_ref, got3_ref, near_ref, basis_ref, slots_ref):
    in_order(sub_ref, [got0_ref, got1_ref, got2_ref, got3_ref], slots_ref, SENT)

    def whole(i, start, size):
        half = slice((i % 2) * ROWS, (i % 2 + 1) * ROWS)
        rows = pl.ds(start + (i // 2) * size, size)
        return jnp.concatenate([slots_ref[s, rows, half] for s in range(SUBS)], axis=1)

    for i in range(LEAVES):
        near_ref[i // 4, pl.ds(i % 4 * PROBES, PROBES), :] = whole(i, 0, PROBES)
        basis_ref[i // 4, pl.ds(i % 4 * RANK, RANK), :] = whole(i, PACKED, RANK)


def weights_kernel(_, couplings_ref, coarse_ref, out_ref):
    for q in range(PARENTS + 1):
        for c in range(4):
            for k in range(0, FAR, 2):
                ref, i = (couplings_ref, 4 * q + c) if q < PARENTS else (coarse_ref, c)
                n = (i * FAR + k) * RANK
                pair = [ref[n : n + RANK], ref[n + RANK : n + 2 * RANK]]
                both = jnp.concatenate(pair, axis=1)
                out_ref[q, pl.ds(c * RANK, RANK), pl.ds(k * RANK, LANES)] = both


def both_halves(row_pair):
    turned = pltpu.roll(row_pair, RANK, 1)
    left = lax.broadcasted_iota(jnp.int32, row_pair.shape, 1) < RANK
    return jnp.where(left, row_pair, turned), jnp.where(left, turned, row_pair)


def unpack_tile(tile, rows_ref, first):
    wide = tile.astype(F32)
    for h in range(2):
        one, two = both_halves(wide[h * OWN : (h + 1) * OWN])
        rows_ref[first + 2 * h] = one
        rows_ref[first + 2 * h + 1] = two


def choose_kernel(asked_ref, got_ref, out_ref, rows_ref):
    for z in range(PLANES):
        for t in range(LEAVES // 4):
            unpack_tile(got_ref[z, t], rows_ref, z * LEAVES + 4 * t)
    left = lax.broadcasted_iota(jnp.int32, (OWN, LANES), 1) < RANK
    for m in range(PLANE):
        for t in range(LEAF_OUT):
            rows = []
            for n in range(4 * t, 4 * t + 4):
                rows.append(rows_ref[n // CAP * LEAVES + asked_ref[m, n]])
            top = jnp.where(left, rows[0], rows[1])
            bottom = jnp.where(left, rows[2], rows[3])
            out_ref[m, t] = jnp.concatenate([top, bottom], axis=0).astype(BF16)
        for z in range(PLANES):
            out_ref[m, LEAF_OUT + z] = got_ref[z, TILES - 1]
        if m % 4 == 3:
            out_ref.send(m // 4)


def far_field(far_ref, coarse_ref, got_ref, weights_ref, transfer_ref, rows_ref):
    for n in range(PLANE * OUT_TILES):
        unpack_tile(got_ref[n], rows_ref, 4 * n)
    rows_ref[GOT_ROWS] = jnp.zeros((OWN, LANES), F32)
    left = lax.broadcasted_iota(jnp.int32, (OWN, LANES), 1) < RANK

    def apply(index_ref, q, weights):
        picked = []
        for c in range(4):
            pairs = []
            for k in range(0, FAR, 2):
                one = rows_ref[index_ref[4 * q + c, k]]
                two = rows_ref[index_ref[4 * q + c, k + 1]]
                pairs.append(jnp.where(left, one, two))
            picked.append(jnp.concatenate(pairs, axis=1))
        picked = jnp.concatenate(picked, axis=0).astype(BF16)
        return diagonal(dot_nt(picked, weights), OWN)

    coarse = apply(coarse_ref, 0, weights_ref[PARENTS]).astype(BF16)
    fields = []
    for q in range(PARENTS):
        down = dot_nt(coarse[:, q * RANK : (q + 1) * RANK], transfer_ref[q])
        fields.append(apply(far_ref, q, weights_ref[q]) + down)
    return fields


def field_kernel(
    far_ref, coarse_ref, got_ref, weights_ref, transfer_ref, out_ref, rows_ref
):
    fields = far_field(far_ref, coarse_ref, got_ref, weights_ref, transfer_ref, rows_ref)
    for q in range(PARENTS):
        out_ref[q] = to_tile(fields[q])


def field_of(field_ref, q):
    tiles = [field_ref[s, q].astype(F32) for s in range(SUBS)]
    field = [jnp.concatenate([t[:OWN], t[OWN:]], axis=1) for t in tiles]
    return spread_diagonal(jnp.concatenate(field, axis=0)).astype(BF16)


def second_kernel(
    sub_ref,
    field0_ref,
    field1_ref,
    field2_ref,
    field3_ref,
    near_ref,
    basis_ref,
    transfer_ref,
    x_ref,
    low_ref,
    high_ref,
    out_ref,
    field_ref,
    four_ref,
):
    in_order(sub_ref, [field0_ref, field1_ref, field2_ref, field3_ref], field_ref, PARENTS)
    own = probes_of(sub_ref[0])
    tiles = []
    parents = []
    for q in range(PARENTS):
        far = dot(field_of(field_ref, q), basis_ref[q])
        x = near_ref[q].astype(F32) + far
        mine = []
        for c in range(4):
            i = 4 * q + c
            four_ref[c] = x[c * PROBES : (c + 1) * PROBES]
            mine.append(four_ref[c, own, :])
            leaf = x[c * PROBES : (c + 1) * PROBES].astype(BF16)
            x_ref[i] = leaf
            if i < REACH:
                low_ref[i] = leaf
            if i >= LEAVES - REACH:
                high_ref[i - (LEAVES - REACH)] = leaf
        x_ref.send(q)
        mine = jnp.concatenate(mine, axis=0).astype(BF16)
        leaf = diagonal(dot_nt(mine, basis_ref[q]), OWN)
        tiles.append(to_tile(leaf))
        parents.append(dot(leaf.astype(BF16), transfer_ref[q]))
    tiles.append(to_tile(jnp.concatenate(parents, axis=1)))
    for t in range(TILES):
        for z in range(PLANES):
            out_ref[z, t] = tiles[t]


def output_kernel(
    sub_ref, field0_ref, field1_ref, field2_ref, field3_ref, near_ref, basis_ref, out_ref, field_ref
):
    in_order(sub_ref, [field0_ref, field1_ref, field2_ref, field3_ref], field_ref, PARENTS)
    outs = []
    for q in range(PARENTS):
        far = dot(field_of(field_ref, q), basis_ref[q])
        for c in range(4):
            outs.append(near_ref[4 * q + c] + far[c * PROBES : (c + 1) * PROBES])
    out_ref[...] = jnp.transpose(jnp.stack(outs), (1, 0, 2)).astype(BF16)


def near_parts(first_ref, list_ref, x_ref, low_ref, high_ref, blocks_ref, wide_ref):
    wide_ref[pl.ds(0, REACH)] = low_ref[...]
    wide_ref[pl.ds(REACH, LEAVES)] = x_ref[...]
    wide_ref[pl.ds(REACH + LEAVES, REACH)] = high_ref[...]
    wide_ref[2 * REACH + LEAVES] = jnp.zeros((PROBES, UNKNOWNS), BF16)

    def of_slot(i, k):
        leaf = list_ref[i, k]
        place = jnp.where(leaf >= 0, leaf - first_ref[0] + REACH, LEAVES + 2 * REACH)
        return wide_ref[place]

    for q in range(PARENTS):
        four = []
        for i in range(4 * q, 4 * q + 4):
            x = jnp.concatenate([of_slot(i, k) for k in range(NEAR)], axis=1)
            starts = [(i * NEAR + k) * ROWS for k in range(NEAR)]
            blocks = jnp.concatenate([blocks_ref[n : n + ROWS] for n in starts], axis=1)
            four.append(dot_nt(x, blocks))
        yield four


def near_sent_kernel(
    first_ref, list_ref, x_ref, low_ref, high_ref, blocks_ref, basis_ref, out_ref, wide_ref
):
    parts = near_parts(first_ref, list_ref, x_ref, low_ref, high_ref, blocks_ref, wide_ref)
    for q, four in enumerate(parts):
        for j in range(2):
            pair = jnp.concatenate(four[2 * j : 2 * j + 2], axis=1).astype(BF16)
            out_ref[pl.ds((2 * q + j) * PROBES, PROBES), :] = pair
    for j in range(LEAVES // 2):
        pair = jnp.concatenate([basis_ref[2 * j], basis_ref[2 * j + 1]], axis=1)
        out_ref[pl.ds(PACKED + j * RANK, RANK), :] = pair


def near_kernel(
    sub_ref, first_ref, list_ref, x_ref, low_ref, high_ref, blocks_ref, out_ref, mine_ref, wide_ref
):
    parts = near_parts(first_ref, list_ref, x_ref, low_ref, high_ref, blocks_ref, wide_ref)
    for q, four in enumerate(parts):
        for c in range(4):
            out_ref[4 * q + c] = four[c]
        out_ref.send(q)
    outs = []
    for i in range(LEAVES):
        x = x_ref[i].astype(F32)
        mine = x[:, :ROWS]
        for s in range(1, SUBS):
            mine = jnp.where(sub_ref[0] == s, x[:, s * ROWS : (s + 1) * ROWS], mine)
        outs.append(mine)
    mine_ref[...] = jnp.transpose(jnp.stack(outs), (1, 0, 2)).astype(BF16)


def local(
    probes,
    near_blocks,
    leaf_cluster_basis,
    transfer,
    couplings,
    coarse_couplings,
    near_list,
    distant_interaction_list,
    coarse_list,
):
    groups = PLANES * PLANE
    in_plane = [[z * PLANE + m for m in range(PLANE)] for z in range(PLANES)]
    along_z = [[z * PLANE + m for z in range(PLANES)] for m in range(PLANE)]
    sub = lax.axis_index("sub").reshape(1)
    first_leaf = (lax.axis_index("leaf") * LEAVES).reshape(1)
    four_transfers = transfer.reshape(PARENTS, BRANCH * RANK, RANK)
    four_bases = leaf_cluster_basis.reshape(PARENTS, BRANCH * RANK, ROWS)

    def over_sub(pieces):
        return [pieces[0]] + [
            lax.ppermute(pieces[k], "sub", [(i, (i + k) % SUBS) for i in range(SUBS)])
            for k in range(1, SUBS)
        ]

    x_shape = (LEAVES, PROBES, UNKNOWNS)
    edge = (REACH, PROBES, UNKNOWNS)
    tile = (16, LANES)
    message = (PLANES, TILES) + tile
    rows_scratch = [pltpu.VMEM((GOT_ROWS + 1, OWN, LANES), F32)]

    wide_scratch = [pltpu.VMEM((LEAVES + 2 * REACH + 1, PROBES, UNKNOWNS), BF16)]

    def halos(low, high):
        from_below = lax.ppermute(high, "leaf", [(i, i + 1) for i in range(groups - 1)])
        from_above = lax.ppermute(low, "leaf", [(i + 1, i) for i in range(groups - 1)])
        return from_below, from_above

    def near_args(x, from_below, from_above, where):
        tables = of_kind("smem", first_leaf) + of_kind("table", near_list)
        blocks = of_kind("cut", near_blocks.reshape(-1, UNKNOWNS))
        return tables + of_kind("hbm", x) + of_kind(where, from_below, from_above) + blocks

    def along(tiles):
        return lax.all_to_all(tiles, "leaf", 0, 0, axis_index_groups=along_z, tiled=True)

    def within(column, asked, edges=()):
        (chosen,) = call(
            choose_kernel,
            "choose_rows",
            [((PLANE, OUT_TILES) + tile, BF16, 2)],
            of_kind("smem", asked) + of_kind("vmem", column),
            [pltpu.VMEM((PLANES * LEAVES, OWN, LANES), F32)],
        )
        chosen, edges = lax.optimization_barrier((chosen, edges))
        got = lax.all_to_all(chosen, "leaf", 0, 0, axis_index_groups=in_plane, tiled=True)
        return got.reshape((PLANE * OUT_TILES,) + tile), edges

    packed = call(
        partial_kernel,
        "partial_sums",
        [((PACKED + TILES * 16, LANES), BF16)] * SUBS,
        of_kind("smem", sub) + of_kind("hbm", probes, four_bases, four_transfers),
        [pltpu.VMEM((TILES, PROBES, 4 * RANK), F32)],
    )
    first_leaf, packed = lax.optimization_barrier((first_leaf, packed))
    wanted, far_index, coarse_index = call(
        index_kernel,
        "index_tables",
        [
            ((PLANE, LANES), jnp.int32),
            (distant_interaction_list.shape, jnp.int32, 1),
            (coarse_list.shape, jnp.int32, 1),
        ],
        of_kind("smem", first_leaf) + of_kind("hbm", distant_interaction_list, coarse_list),
    )
    pieces, wanted = lax.optimization_barrier((over_sub(packed), wanted))
    x0, low, high, tiles = call(
        first_kernel,
        "first_coefficients",
        [(x_shape, BF16, 1), (edge, BF16), (edge, BF16), (message, BF16, 1)],
        of_kind("smem", sub) + of_kind("vmem", *pieces),
        [pltpu.VMEM((SUBS, PACKED, LANES), BF16)],
    )
    column, wanted = lax.optimization_barrier((along(tiles), wanted))
    asked = lax.all_to_all(wanted, "leaf", 0, 0, axis_index_groups=in_plane, tiled=True)
    (sent,) = call(
        near_sent_kernel,
        "near_field_sent",
        [((SENT, LANES), BF16, 1)],
        near_args(x0, *halos(low, high), "vmem") + of_kind("hbm", leaf_cluster_basis),
        wide_scratch,
    )
    column, sent, later = lax.optimization_barrier((column, sent, sub))
    got, _ = within(column, asked)
    (weights,) = call(
        weights_kernel,
        "join_couplings",
        [((PARENTS + 1, 4 * RANK, FAR * RANK), BF16)],
        of_kind("smem", later) + of_kind("cut", couplings.reshape(-1, RANK), coarse_couplings.reshape(-1, RANK)),
    )

    def far(got):
        (field,) = call(
            field_kernel,
            "far_field",
            [((PARENTS,) + tile, BF16)],
            of_kind("table", far_index, coarse_index)
            + of_kind("vmem", got, weights, four_transfers),
            rows_scratch,
        )
        return field

    field_scratch = pltpu.VMEM((SUBS, PARENTS) + tile, BF16)
    field1, pieces = far(got), over_sub([sent] * SUBS)
    near1, basis = call(
        join_kernel,
        "join_near_basis",
        [((PARENTS, 4 * PROBES, UNKNOWNS), BF16), ((PARENTS, 4 * RANK, UNKNOWNS), BF16)],
        of_kind("smem", sub) + of_kind("hbm", pieces[0]) + of_kind("any", *pieces[1:]),
        [pltpu.VMEM((SUBS, SENT, LANES), BF16)],
    )
    x1, low, high, tiles = call(
        second_kernel,
        "second_coefficients",
        [(x_shape, BF16, 4), (edge, BF16), (edge, BF16), (message, BF16, 1)],
        of_kind("smem", sub)
        + of_kind("vmem", *over_sub([field1] * SUBS))
        + of_kind("vmem", near1, basis, four_transfers),
        [field_scratch, pltpu.VMEM((4, PROBES, UNKNOWNS), F32)],
    )
    got, edges = within(along(tiles), asked, halos(low, high))
    near2, first = call(
        near_kernel,
        "near_field",
        [((LEAVES, PROBES, ROWS), F32, 4), (probes.shape, BF16)],
        of_kind("smem", sub) + near_args(x1, *edges, "hbm"),
        wide_scratch,
    )
    got, near2 = lax.optimization_barrier((got, near2))
    (second_apply,) = call(
        output_kernel,
        "output",
        [(probes.shape, BF16)],
        of_kind("smem", sub)
        + of_kind("vmem", *over_sub([far(got)] * SUBS))
        + of_kind("hbm", near2)
        + of_kind("vmem", four_bases),
        [field_scratch],
    )
    return (first, second_apply)


def solution(mesh):
    return jax.shard_map(
        local,
        mesh=mesh,
        in_specs=(
            P(None, "leaf", "sub"),
            P("leaf", None, "sub", None),
            P("leaf", None, "sub"),
            P("leaf", None, None),
            P("leaf", None, None, None),
            P("leaf", None, None, None),
            P("leaf", None),
            P("leaf", None),
            P("leaf", None),
        ),
        out_specs=(P(None, "leaf", "sub"), P(None, "leaf", "sub")),
        check_vma=False,
    )
```
